256 devices in a mesh: section: 16 (over z, core), fsdp: 16 (over y, x).
Axes of the slice: x: 4, y: 4, z: 8, core: 2. Of those that a mesh axis runs over, the one named last changes fastest.
Arguments:
- tokens: bfloat16 [16, 2048, 5120], P('section', 'fsdp'), may hold values from -60 to 60
- cotangents: bfloat16 [16, 2048, 1024], P('section', 'fsdp'), may hold values from -6 to 6
- norm_gain: float32 [16, 5120], P('section'), may hold values from 0.1 to 1.9
- master: float32 [16, 5120, 1024], P('section', 'fsdp'), may hold values from -5 to 5
- moment: float32 [16, 5120, 1024], P('section', 'fsdp'), may hold values from -4 to 4
- second: float32 [16, 5120, 1024], P('section', 'fsdp'), may hold values from 0.05 to 2
- head_owner: int32 [16, 4], P('section'), may hold values from 0 to 3, each once within a row
- plan: int32 [4], replicated, may hold values from 0 to 3, each once
Outputs:
- input_grads: bfloat16 [16, 2048, 5120], P('section', 'fsdp')
- moment_new: float32 [16, 5120, 1024], P('section', 'fsdp')
- second_new: float32 [16, 5120, 1024], P('section', 'fsdp')
- rollout: bfloat16 [16, 1024, 5120], P('section', 'fsdp')
The draws below stay inside these ranges and needn't reach their ends.
Inputs may be any that keep to these rules, and one draw needn't show every extreme that they name: `head_owner`: each row lists every head once. `plan`: every slot is named once.
All inputs are finite; a program needn't handle non-finite values.
Results may differ from the reference program's by a relative error of at most 0.011.
Values may be sent and summed in bfloat16 or wider, within the bound.
A program may use at most 192 MiB of HBM per device.

```python
import math
import jax
import jax.numpy as jnp
from jax import lax

D = 5120
HEAD = 128
KV_HEADS = 4
MICRO = 4
TOK_DEV = 128
KVC = 1024
TOKENS = 2048
LAYERS = 16
N_FSDP = 16


def draw_tokens(key, part):
    key = jax.random.fold_in(key, 11)
    base_key, row_key, col_key = jax.random.split(key, 3)
    raw_values = jnp.clip(jax.random.normal(base_key, (LAYERS, TOKENS, D), jnp.float32), -5.0, 5.0)
    row_scale = jnp.exp(jax.random.uniform(row_key, (LAYERS, TOKENS, 1), jnp.float32, 0.0, math.log(10.0))) * 0.4
    col_scale = jnp.exp(jax.random.uniform(col_key, (LAYERS, 1, D), jnp.float32, 0.0, math.log(10.0))) * 0.3
    return (raw_values * row_scale * col_scale).astype(jnp.bfloat16)


def level_of(stream_key, extent, cuts, low, top_value):
    def one(position, parts):
        steps = jax.random.uniform(jax.random.fold_in(jax.random.fold_in(stream_key, 6), position), (parts,), jnp.float32, low / len(cuts), top_value / len(cuts))
        return jnp.repeat(jnp.exp(steps), extent[position] // parts).reshape((-1,) + (1,) * (len(extent) - position - 1))

    gain = one(*cuts[0])
    for cut in cuts[1:]:
        gain = gain * one(*cut)
    return gain


def scatter_about(key, dims, scale, reach, pieces=(), kind=jnp.bfloat16):
    loudness = level_of(key, dims, pieces, -0.22, 0.18) if pieces else 1.0
    drawn = jax.random.normal(key, dims, jnp.float32) * scale * loudness
    return jnp.minimum(jnp.maximum(drawn, -reach), reach).astype(kind)


def setup_inputs(seed: int = 0) -> dict:
    keys = jax.random.split(jax.random.key(seed), 9)
    tokens = draw_tokens(jax.random.fold_in(keys[8], 71), 0)
    cotangents = scatter_about(keys[1], (LAYERS, TOKENS, KVC), 1.0, 6.0, ((0, 16), (1, 16)))
    norm_gain = jnp.clip(1.0 + 0.18 * jax.random.normal(keys[2], (LAYERS, D), jnp.float32), 0.1, 1.9)
    master = scatter_about(keys[3], (LAYERS, D, KVC), 1.0, 5.0, ((0, 16), (1, 16)), jnp.float32)
    moment = scatter_about(keys[4], (LAYERS, D, KVC), 0.3, 4.0, ((0, 16), (1, 16)), jnp.float32)
    second = jnp.clip(jnp.exp(math.log(2.0) - 3.6888794 * jax.random.uniform(keys[5], (LAYERS, D, KVC), jnp.float32) ** level_of(keys[5], (LAYERS, D, KVC), ((0, 16), (1, 16)), -0.2, 0.2)), 0.05, 2.0)
    head_owner = jax.vmap(lambda own: jax.random.permutation(own, KV_HEADS))(jax.random.split(keys[6], LAYERS)).reshape((LAYERS, KV_HEADS)).astype(jnp.int32)
    plan = jax.random.permutation(keys[7], MICRO).astype(jnp.int32)
    return {"tokens": tokens, "cotangents": cotangents, "norm_gain": norm_gain, "master": master, "moment": moment, "second": second, "head_owner": head_owner, "plan": plan}


beta_one = 0.9
beta_two = 0.95
bias_one = 1.0 - 0.9 ** 10
bias_two = 1.0 - 0.95 ** 10
adam_eps = 1e-08
learn_rate = 0.02
weight_decay = 0.1
norm_eps = 1e-06

def input_term(widened, inverse, gain_row, spread):
    scaled = spread * gain_row
    mean_term = lax.optimization_barrier(jnp.mean(scaled * widened, axis=-1, keepdims=True))
    return inverse * scaled - widened * inverse * inverse * inverse * mean_term

def adam_step(master, moment, second, gradient):
    moment_new = beta_one * moment + (1.0 - beta_one) * gradient
    second_new = beta_two * second + (1.0 - beta_two) * gradient * gradient
    update = moment_new / bias_one / (jnp.sqrt(second_new / bias_two) + adam_eps)
    weights = master - learn_rate * (update + weight_decay * master)
    return (moment_new, second_new, weights)

def reference(tokens, cotangents, norm_gain, master, moment, second, head_owner, plan):
    proj_scale = D ** (-0.5)

    def one_layer(running, layer_items):
        tok_rows, cot_rows, gain_row, master_rows, moment_rows, second_rows, owner_row = layer_items
        blocks = cot_rows.reshape(N_FSDP, MICRO, TOK_DEV // MICRO, KVC)
        ordered = jnp.take(blocks, plan, axis=1).reshape(TOKENS, KVC)
        widened = tok_rows.astype(jnp.float32)
        inverse = lax.rsqrt(lax.optimization_barrier(jnp.mean(widened * widened, axis=-1, keepdims=True)) + norm_eps)
        normed = (widened * inverse * gain_row).astype(jnp.bfloat16)
        low_weights = master_rows.astype(jnp.bfloat16)
        spread = jnp.dot(ordered, low_weights.T, preferred_element_type=jnp.float32) * proj_scale
        own_term = input_term(widened, inverse, gain_row, spread)

        def shard_grad(running_grad, shard_pair):
            normed_shard, cot_shard = shard_pair
            partial_term = jnp.dot(normed_shard.T, cot_shard, preferred_element_type=jnp.float32) * proj_scale
            rounded = lax.optimization_barrier(partial_term.astype(jnp.bfloat16))
            return (running_grad + rounded.astype(jnp.float32), None)
        gradient, _ = lax.scan(shard_grad, jnp.zeros((D, KVC), jnp.float32), (normed.reshape(N_FSDP, TOK_DEV, D), ordered.reshape(N_FSDP, TOK_DEV, KVC)))
        moment_new, second_new, weights = adam_step(master_rows, moment_rows, second_rows, gradient)
        by_head = weights.astype(jnp.bfloat16).reshape(D, 2, KV_HEADS, HEAD)
        placed = jnp.take(by_head, owner_row, axis=2)
        rollout = jnp.transpose(placed, (2, 1, 3, 0)).reshape(KVC, D)
        summed = running + own_term
        return (summed, (summed.astype(jnp.bfloat16), moment_new, second_new, rollout))
    _, outputs = lax.scan(one_layer, jnp.zeros((TOKENS, D), jnp.float32), (tokens, cotangents, norm_gain, master, moment, second, head_owner), reverse=True)
    return (outputs[0], outputs[1], outputs[2], outputs[3])
```

```python
import functools

import jax
import jax.numpy as jnp
from jax import lax
from jax.experimental import pallas as pl
from jax.experimental.pallas import tpu as pltpu
from jax.sharding import PartitionSpec as P

beta_one = 0.9
beta_two = 0.95
bias_one = 1.0 - 0.9**10
bias_two = 1.0 - 0.95**10
adam_eps = 1e-08
learn_rate = 0.02
weight_decay = 0.1
norm_eps = 1e-06

MESH = pl.DeviceIdType.MESH
F32 = jnp.float32
BF16 = jnp.bfloat16

D = 5120
C = 1024
T = 128
R = 320
H = R // 2
QD = D // 4
HD = D // 2
MB = 32
NMB = 4
CH = 16
NCH = T // CH
RO = 64


def kernel(
    tok_hbm, cot_hbm, gain, mas_hbm, mom_hbm, sec_hbm, owner, plan,
    ig_hbm, mn_hbm, sn_hbm, ro_hbm,
    tok, cot, mas, mom, sec,
    wg, g, xs, xr, ss, sr, inv,
    pf, s_opp, s_right, s_left, o_left, o_right, r_left, r_right,
    wnew, rs, rr, ro,
    own, es, er, us, ur, mr, out,
    in_sem, out_sem, og_sem,
    w_ss, w_rs, g_ss, g_rs, x_ss, x_rs, s_ss, s_rs, p_ss, p_rs, r_ss, r_rs,
    e_ss, e_rs, u_ss, u_rs, m_ss, m_rs,
):
    s = lax.axis_index("section")
    f = lax.axis_index("fsdp")
    z, c = s // 2, s % 2
    y, x = f // 4, f % 4

    def at_x(d):
        return (s, y * 4 + lax.rem(x + d, 4))

    def at_y(d):
        return (s, lax.rem(y + d, 4) * 4 + x)

    partner = (z * 2 + 1 - c, f)
    below = (lax.rem(z + 7, 8) * 2 + c, f)
    above = (lax.rem(z + 1, 8) * 2 + c, f)

    def send(src, dst, ssem, rsem, dev):
        return pltpu.make_async_remote_copy(
            src_ref=src, dst_ref=dst, send_sem=ssem, recv_sem=rsem, device_id=dev, device_id_type=MESH
        )

    loads = [
        pltpu.make_async_copy(a, b, in_sem.at[i])
        for i, (a, b) in enumerate(
            [(mas_hbm, mas), (cot_hbm, cot), (tok_hbm, tok), (mom_hbm, mom), (sec_hbm, sec)]
        )
    ]
    for ld in loads:
        ld.start()

    bar = pltpu.get_barrier_semaphore()
    for k in range(1, 16):
        pl.semaphore_signal(bar, inc=1, device_id=(s, lax.rem(f + k, 16)), device_id_type=MESH)
    for dev in (partner, below, above):
        pl.semaphore_signal(bar, inc=1, device_id=dev, device_id_type=MESH)

    @pl.when(z == 7)
    def _():
        ur[...] = jnp.zeros_like(ur)

    def w_rows(block, half):
        return pl.ds(pl.multiple_of(block * R + half * H, 32), H)

    loads[0].wait()
    wg[pl.ds(pl.multiple_of(x * R, 32), R), :] = mas[...].astype(BF16)

    loads[1].wait()
    for i in range(NMB):
        p = plan[i]
        v = cot[0:MB, :]
        for j in range(1, NMB):
            v = jnp.where(p == j, cot[j * MB : (j + 1) * MB, :], v)
        g[0, i * MB : (i + 1) * MB, :] = v

    pl.semaphore_wait(bar, 18)

    w_out = []
    for n, (dev, half) in enumerate([(1, 0), (3, 1), (1, 1), (3, 0)]):
        rows = w_rows(x, half)
        w_out.append(send(wg.at[rows], wg.at[rows], w_ss.at[n], w_rs.at[n], at_x(dev)))
    for cp in w_out:
        cp.start()

    g_out = []
    hg = T // 2
    for n, (dev, half) in enumerate([(1, 0), (3, 1), (1, 1), (3, 0)]):
        rows = pl.ds(half * hg, hg)
        g_out.append(send(g.at[0, rows], g.at[dev, rows], g_ss.at[n], g_rs.at[n], at_y(dev)))
    for cp in g_out:
        cp.start()

    loads[2].wait()

    def norm_chunk(k, carry):
        rows = pl.ds(pl.multiple_of(k * CH, CH), CH)
        acc = jnp.zeros((CH, 1), F32)
        for b in range(4):
            v = tok[rows, b * QD : (b + 1) * QD].astype(F32)
            acc = acc + jnp.sum(v * v, axis=-1, keepdims=True)
        iv = lax.rsqrt(acc * (1.0 / D) + norm_eps)
        inv[rows, :] = jnp.broadcast_to(iv, (CH, 128))
        for b in range(4):
            v = tok[rows, b * QD : (b + 1) * QD].astype(F32)
            xs[b, rows, :] = (v * iv * gain[:, b * QD : (b + 1) * QD]).astype(BF16)
        return carry

    lax.fori_loop(0, NCH, norm_chunk, 0)

    x_out = []
    for n, dev in enumerate([2, 1, 3]):
        x_out.append(
            send(xs.at[lax.rem(y + dev, 4)], xr.at[dev], x_ss.at[n], x_rs.at[n], at_y(dev))
        )
    for cp in x_out:
        cp.start()
    xr[0] = xs[y]

    g_out[0].wait_recv()
    rows0, rows1 = pl.ds(0, hg), pl.ds(hg, hg)
    g_fwd = [send(g.at[1, rows0], g.at[2, rows0], g_ss.at[4], g_rs.at[4], at_y(1))]
    g_fwd[0].start()
    g_out[1].wait_recv()
    g_fwd.append(send(g.at[3, rows1], g.at[2, rows1], g_ss.at[5], g_rs.at[5], at_y(3)))
    g_fwd[1].start()

    w_out[0].wait_recv()
    rows = w_rows(lax.rem(x + 3, 4), 0)
    w_fwd = [send(wg.at[rows], wg.at[rows], w_ss.at[4], w_rs.at[4], at_x(1))]
    w_fwd[0].start()
    w_out[1].wait_recv()
    rows = w_rows(lax.rem(x + 1, 4), 1)
    w_fwd.append(send(wg.at[rows], wg.at[rows], w_ss.at[5], w_rs.at[5], at_x(3)))
    w_fwd[1].start()

    for cp in (g_out[2], g_out[3], g_fwd[0], g_fwd[1]):
        cp.wait_recv()
    for cp in (w_out[2], w_out[3], w_fwd[0], w_fwd[1]):
        cp.wait_recv()

    proj_scale = D ** (-0.5)
    sr_out = []

    for i in range(NMB):
        rows = pl.ds(i * MB, MB)
        lhs = jnp.concatenate([g[r, i * MB : (i + 1) * MB, :] for r in range(4)], axis=0)
        for q in range(5):
            cols = slice(q * 256, (q + 1) * 256)
            v = (
                lax.dot_general(
                    lhs, wg[q * 256 : (q + 1) * 256, :], (((1,), (1,)), ((), ())),
                    preferred_element_type=F32,
                )
                * proj_scale
            ).astype(BF16)
            for r in range(1, 4):
                ss[r, i * MB : (i + 1) * MB, cols] = v[r * MB : (r + 1) * MB]
            sr[y, i * MB : (i + 1) * MB, cols] = v[0:MB]
        for n, r in enumerate([2, 1, 3]):
            cp = send(ss.at[r, rows], sr.at[y, rows], s_ss.at[i, n], s_rs.at[i, n], at_y(4 - r))
            cp.start()
            sr_out.append(cp)

    for cp in x_out:
        cp.wait_recv()
    gall = g[...].reshape(4 * T, C)
    for q in range(5):
        lhs = jnp.concatenate([xr[r, :, q * 256 : (q + 1) * 256] for r in range(4)], axis=0)
        pf[q * 256 : (q + 1) * 256, :] = (
            lax.dot_general(lhs, gall, (((0,), (0,)), ((), ())), preferred_element_type=F32)
            * proj_scale
        )

    def p_rows(d, half):
        return pf[pl.ds(pl.multiple_of(lax.rem(x + d, 4) * R + half * H, 32), H), :]

    s_opp[0:H, :] = p_rows(2, 0).astype(BF16)
    s_opp[H:R, :] = p_rows(2, 1).astype(BF16)
    p_out = [
        send(s_opp.at[pl.ds(0, H)], o_left, p_ss.at[0], p_rs.at[0], at_x(1)),
        send(s_opp.at[pl.ds(H, H)], o_right, p_ss.at[1], p_rs.at[1], at_x(3)),
    ]
    for cp in p_out:
        cp.start()
    s_right[H:R, :] = p_rows(1, 1).astype(BF16)
    s_left[0:H, :] = p_rows(3, 0).astype(BF16)
    p_out += [
        send(s_right.at[pl.ds(H, H)], r_left.at[pl.ds(H, H)], p_ss.at[2], p_rs.at[2], at_x(1)),
        send(s_left.at[pl.ds(0, H)], r_right.at[pl.ds(0, H)], p_ss.at[3], p_rs.at[3], at_x(3)),
    ]
    for cp in p_out[2:]:
        cp.start()
    p_out += [
        send(s_right.at[pl.ds(0, H)], r_left.at[pl.ds(0, H)], p_ss.at[4], p_rs.at[4], at_x(1)),
        send(s_left.at[pl.ds(H, H)], r_right.at[pl.ds(H, H)], p_ss.at[5], p_rs.at[5], at_x(3)),
    ]

    def reduce_forward():
        p_out[0].wait_recv()
        s_right[0:H, :] = (p_rows(1, 0) + o_left[...].astype(F32)).astype(BF16)
        p_out[4].start()
        p_out[1].wait_recv()
        s_left[H:R, :] = (p_rows(3, 1) + o_right[...].astype(F32)).astype(BF16)
        p_out[5].start()

    mn_copy = pltpu.make_async_copy(mom, mn_hbm, out_sem.at[0])
    sn_copy = pltpu.make_async_copy(sec, sn_hbm, out_sem.at[1])
    ro_copy = pltpu.make_async_copy(ro, ro_hbm, out_sem.at[2])

    r_out = [
        send(
            rs.at[lax.rem(f + k, 16)], rr.at[f], r_ss.at[k - 1], r_rs.at[k - 1],
            (s, lax.rem(f + k, 16)),
        )
        for k in range(1, 16)
    ]

    def update():
        for cp in p_out[2:]:
            cp.wait_recv()
        loads[3].wait()
        loads[4].wait()

        def adam(k, carry):
            rows = pl.ds(pl.multiple_of(k * 32, 32), 32)
            grad = (
                pf[pl.ds(pl.multiple_of(x * R + k * 32, 32), 32), :]
                + r_left[rows, :].astype(F32)
                + r_right[rows, :].astype(F32)
            )
            m = beta_one * mom[rows, :] + (1.0 - beta_one) * grad
            v = beta_two * sec[rows, :] + (1.0 - beta_two) * grad * grad
            mom[rows, :] = m
            sec[rows, :] = v
            step = m * (1.0 / bias_one) / (jnp.sqrt(v * (1.0 / bias_two)) + adam_eps)
            old = mas[rows, :]
            wnew[rows, :] = (old - learn_rate * (step + weight_decay * old)).astype(BF16)
            return carry

        lax.fori_loop(0, R // 32, adam, 0)
        mn_copy.start()
        sn_copy.start()

        ia = lax.broadcasted_iota(jnp.int32, (128, 128), 0)
        ib = lax.broadcasted_iota(jnp.int32, (128, 128), 1)
        eye = jnp.where(ia == ib, 1.0, 0.0).astype(BF16)
        for j in range(4):
            o = owner[j]
            for p in range(2):
                v = wnew[:, p * 512 : p * 512 + 128]
                for h in range(1, 4):
                    v = jnp.where(o == h, wnew[:, p * 512 + h * 128 : p * 512 + (h + 1) * 128], v)
                t = lax.dot_general(
                    eye, v, (((1,), (1,)), ((), ())), preferred_element_type=F32
                ).astype(BF16)
                rs[j * 4 + p * 2] = t[0:RO]
                rs[j * 4 + p * 2 + 1] = t[RO : 2 * RO]
        for cp in r_out:
            cp.start()
        rr[f] = rs[f]

    def chain_rows(k):
        return pl.ds(pl.multiple_of(k * CH, CH), CH)

    def e_copy(k):
        rows = chain_rows(k)
        return send(es.at[:, rows], er.at[:, rows], e_ss.at[k], e_rs.at[k], partner)

    def u_copy(k, q):
        rows = chain_rows(k)
        return send(us.at[q, rows], ur.at[q, rows], u_ss.at[k, q], u_rs.at[k, q], below)

    def m_copy(k, q, ref):
        rows = chain_rows(k)
        return send(ref.at[q, rows], mr.at[q, rows], m_ss.at[k, q], m_rs.at[k, q], partner)

    def og_copy(k):
        rows = chain_rows(k)
        return [
            pltpu.make_async_copy(
                out.at[b, rows], ig_hbm.at[rows, pl.ds(b * QD, QD)], og_sem.at[k, b]
            )
            for b in range(4)
        ]

    def finish(k):
        rows = chain_rows(k)
        for q in range(2):
            m_copy(k, q, us).wait_recv()
            b = (1 - c) * 2 + q
            m = mr[q, rows, :].astype(F32)
            out[b, rows, :] = jnp.where(c == 1, m + own[b, rows, :], m).astype(BF16)
        for cp in og_copy(k):
            cp.start()

    def chain_step(k, first):
        rows = chain_rows(k)
        acc = jnp.zeros((CH, 1), F32)
        for b in range(4):
            t = tok[rows, b * QD : (b + 1) * QD].astype(F32)
            sc = sr[b, rows, :].astype(F32) * gain[:, b * QD : (b + 1) * QD]
            acc = acc + jnp.sum(sc * t, axis=-1, keepdims=True)
        iv = inv[rows, 0:1]
        coef = iv * iv * iv * (acc * (1.0 / D))
        for b in range(4):
            t = tok[rows, b * QD : (b + 1) * QD].astype(F32)
            sc = sr[b, rows, :].astype(F32) * gain[:, b * QD : (b + 1) * QD]
            own[b, rows, :] = iv * sc - t * coef
        for q in range(2):
            es[q, rows, :] = own[(1 - c) * 2 + q, rows, :].astype(BF16)
        e_copy(k).start()
        e_copy(k).wait_recv()
        for q in range(2):

            @pl.when(z < 7)
            def _():
                u_copy(k, q).wait_recv()

            b = c * 2 + q
            u = ur[q, rows, :].astype(F32)
            mine = u + own[b, rows, :]
            un = mine + er[q, rows, :].astype(F32)
            unb = un.astype(BF16)
            us[q, rows, :] = unb

            @pl.when(z > 0)
            def _():
                u_copy(k, q).start()

            @pl.when(c == 0)
            def _():
                m_copy(k, q, ur).start()

            @pl.when(c == 1)
            def _():
                m_copy(k, q, us).start()

            out[b, rows, :] = jnp.where(c == 1, mine.astype(BF16), unb)

        if not first:
            finish(k - 1)

    fwd_slot = jnp.where(z == 7, 1, 0)
    upd_slot = jnp.minimum(z, 4)

    for i in range(NMB + 1):

        @pl.when(fwd_slot == i)
        def _():
            reduce_forward()

        @pl.when(upd_slot == i)
        def _():
            update()

        if i < NMB:
            for n in range(3):
                sr_out[i * 3 + n].wait_recv()
            for h in range(MB // CH):
                k = i * (MB // CH) + h
                chain_step(k, k == 0)
    finish(NCH - 1)

    for cp in r_out:
        cp.wait_recv()
    for i in range(8):
        ro[:, i * 2 * R : (i + 1) * 2 * R] = jnp.concatenate([rr[2 * i], rr[2 * i + 1]], axis=1)
    ro_copy.start()

    for cp in w_out + w_fwd + g_out + g_fwd + x_out + sr_out + p_out + r_out:
        cp.wait_send()

    def drain(k, carry):
        e_copy(k).wait_send()
        for q in range(2):
            m_copy(k, q, us).wait_send()

            @pl.when(z > 0)
            def _():
                u_copy(k, q).wait_send()

        for cp in og_copy(k):
            cp.wait()
        return carry

    lax.fori_loop(0, NCH, drain, 0)
    mn_copy.wait()
    sn_copy.wait()
    ro_copy.wait()


def shards(tokens, cotangents, norm_gain, master, moment, second, head_owner, plan):
    hbm = pl.BlockSpec(memory_space=pl.ANY)
    vmem = pl.BlockSpec(memory_space=pltpu.VMEM)
    smem = pl.BlockSpec(memory_space=pltpu.SMEM)
    V = pltpu.VMEM
    dma = pltpu.SemaphoreType.DMA
    scratch = [
        V((T, D), BF16), V((T, C), BF16), V((R, C), F32), V((R, C), F32), V((R, C), F32),
        V((4 * R, C), BF16), V((4, T, C), BF16), V((4, T, QD), BF16), V((4, T, QD), BF16),
        V((4, T, QD), BF16), V((4, T, QD), BF16), V((T, 128), F32),
        V((4 * R, C), F32), V((R, C), BF16), V((R, C), BF16), V((R, C), BF16),
        V((H, C), BF16), V((H, C), BF16), V((R, C), BF16), V((R, C), BF16),
        V((R, C), BF16), V((16, RO, R), BF16), V((16, RO, R), BF16), V((RO, D), BF16),
        V((4, T, QD), F32), V((2, T, QD), BF16), V((2, T, QD), BF16), V((2, T, QD), BF16),
        V((2, T, QD), BF16), V((2, T, QD), BF16), V((4, T, QD), BF16),
        dma((5,)), dma((3,)), dma((NCH, 4)),
        dma((6,)), dma((6,)), dma((6,)), dma((6,)), dma((3,)), dma((3,)),
        dma((NMB, 3)), dma((NMB, 3)), dma((6,)), dma((6,)), dma((15,)), dma((15,)),
        dma((NCH,)), dma((NCH,)), dma((NCH, 2)), dma((NCH, 2)), dma((NCH, 2)), dma((NCH, 2)),
    ]
    ig, mn, sn, ro = pl.pallas_call(
        kernel,
        out_shape=(
            jax.ShapeDtypeStruct((T, D), BF16),
            jax.ShapeDtypeStruct((R, C), F32),
            jax.ShapeDtypeStruct((R, C), F32),
            jax.ShapeDtypeStruct((RO, D), BF16),
        ),
        in_specs=[hbm, hbm, vmem, hbm, hbm, hbm, smem, smem],
        out_specs=(hbm, hbm, hbm, hbm),
        scratch_shapes=scratch,
        name="layer_backward",
        cost_estimate=pl.CostEstimate(
            flops=4 * T * C * D, bytes_accessed=12_000_000, transcendentals=2 * R * C
        ),
        compiler_params=pltpu.CompilerParams(
            collective_id=0, has_side_effects=True, vmem_limit_bytes=56 * 1024 * 1024
        ),
    )(tokens[0], cotangents[0], norm_gain, master[0], moment[0], second[0], head_owner[0], plan)
    return (ig[None], mn[None], sn[None], ro[None])


def solution(mesh):
    in_specs = (
        P("section", "fsdp", None),
        P("section", "fsdp", None),
        P("section", None),
        P("section", "fsdp", None),
        P("section", "fsdp", None),
        P("section", "fsdp", None),
        P("section", None),
        P(),
    )
    out_specs = (
        P("section", "fsdp", None),
        P("section", "fsdp", None),
        P("section", "fsdp", None),
        P("section", "fsdp", None),
    )
    return jax.shard_map(shards, mesh=mesh, in_specs=in_specs, out_specs=out_specs, check_vma=False)
```

```python
import functools

import jax
import jax.numpy as jnp
from jax import lax
from jax.experimental import pallas as pl
from jax.experimental.pallas import tpu as pltpu
from jax.sharding import PartitionSpec as P

beta_one = 0.9
beta_two = 0.95
bias_one = 1.0 - 0.9**10
bias_two = 1.0 - 0.95**10
adam_eps = 1e-08
learn_rate = 0.02
weight_decay = 0.1
norm_eps = 1e-06

MESH = pl.DeviceIdType.MESH
F32 = jnp.float32
BF16 = jnp.bfloat16

D = 5120
C = 1024
T = 128
R = 320
H = R // 2
QD = D // 4
HD = D // 2
MB = 32
NMB = 4
CH = 16
NCH = T // CH
HOP = 2
FORWARD_SLOT = 4
UPDATE_SLOT = 10
LAND = 1
RO = 64


def kernel(
    tok_hbm, cot_hbm, gain, mas_hbm, mom_hbm, sec_hbm, owner, plan,
    ig_hbm, mn_hbm, sn_hbm, ro_hbm,
    tok, cot, mas, mom, sec,
    wg, g, xs, xr, ss, sr, inv,
    pf, s_opp, s_right, s_left, o_left, o_right, r_left, r_right,
    wnew, rs, rr, ro,
    own, es, er, ds, dr, us, ur, ls, lr, ms, mr, out,
    in_sem, out_sem, og_sem,
    w_ss, w_rs, g_ss, g_rs, x_ss, x_rs, s_ss, s_rs, p_ss, p_rs, r_ss, r_rs,
    e_ss, e_rs, d_ss, d_rs, u_ss, u_rs, l_ss, l_rs, m_ss, m_rs,
):
    s = lax.axis_index("section")
    f = lax.axis_index("fsdp")
    z, c = s // 2, s % 2
    y, x = f // 4, f % 4

    def at_x(d):
        return (s, y * 4 + lax.rem(x + d, 4))

    def at_y(d):
        return (s, lax.rem(y + d, 4) * 4 + x)

    partner = (z * 2 + 1 - c, f)
    below = (lax.rem(z + 7, 8) * 2 + c, f)
    above = (lax.rem(z + 1, 8) * 2 + c, f)

    def send(src, dst, ssem, rsem, dev):
        return pltpu.make_async_remote_copy(
            src_ref=src, dst_ref=dst, send_sem=ssem, recv_sem=rsem, device_id=dev, device_id_type=MESH
        )

    loads = [
        pltpu.make_async_copy(a, b, in_sem.at[i])
        for i, (a, b) in enumerate(
            [(mas_hbm, mas), (cot_hbm, cot), (tok_hbm, tok), (mom_hbm, mom), (sec_hbm, sec)]
        )
    ]
    for ld in loads:
        ld.start()

    bar = pltpu.get_barrier_semaphore()
    for k in range(1, 16):
        pl.semaphore_signal(bar, inc=1, device_id=(s, lax.rem(f + k, 16)), device_id_type=MESH)
    for dev in (partner, below, above):
        pl.semaphore_signal(bar, inc=1, device_id=dev, device_id_type=MESH)

    for top, ref in ((7, dr), (4, ur), (3, lr)):

        @pl.when(z == top)
        def _():
            ref[...] = jnp.zeros_like(ref)

    def w_rows(block, half):
        return pl.ds(pl.multiple_of(block * R + half * H, 32), H)

    loads[0].wait()
    wg[pl.ds(pl.multiple_of(x * R, 32), R), :] = mas[...].astype(BF16)

    loads[1].wait()
    for i in range(NMB):
        p = plan[i]
        v = cot[0:MB, :]
        for j in range(1, NMB):
            v = jnp.where(p == j, cot[j * MB : (j + 1) * MB, :], v)
        g[0, i * MB : (i + 1) * MB, :] = v

    pl.semaphore_wait(bar, 18)

    w_out = []
    for n, (dev, half) in enumerate([(1, 0), (3, 1), (1, 1), (3, 0)]):
        rows = w_rows(x, half)
        w_out.append(send(wg.at[rows], wg.at[rows], w_ss.at[n], w_rs.at[n], at_x(dev)))
    for cp in w_out:
        cp.start()

    g_out = []
    hg = T // 2
    for n, (dev, half) in enumerate([(1, 0), (3, 1), (1, 1), (3, 0)]):
        rows = pl.ds(half * hg, hg)
        g_out.append(send(g.at[0, rows], g.at[dev, rows], g_ss.at[n], g_rs.at[n], at_y(dev)))
    for cp in g_out:
        cp.start()

    loads[2].wait()

    def norm_chunk(k, carry):
        rows = pl.ds(pl.multiple_of(k * CH, CH), CH)
        acc = jnp.zeros((CH, 1), F32)
        for b in range(4):
            v = tok[rows, b * QD : (b + 1) * QD].astype(F32)
            acc = acc + jnp.sum(v * v, axis=-1, keepdims=True)
        iv = lax.rsqrt(acc * (1.0 / D) + norm_eps)
        inv[rows, :] = jnp.broadcast_to(iv, (CH, 128))
        for b in range(4):
            v = tok[rows, b * QD : (b + 1) * QD].astype(F32)
            xs[b, rows, :] = (v * iv * gain[:, b * QD : (b + 1) * QD]).astype(BF16)
        return carry

    lax.fori_loop(0, NCH, norm_chunk, 0)

    x_out = []
    for n, dev in enumerate([2, 1, 3]):
        x_out.append(
            send(xs.at[lax.rem(y + dev, 4)], xr.at[dev], x_ss.at[n], x_rs.at[n], at_y(dev))
        )
    for cp in x_out:
        cp.start()
    xr[0] = xs[y]

    g_out[0].wait_recv()
    rows0, rows1 = pl.ds(0, hg), pl.ds(hg, hg)
    g_fwd = [send(g.at[1, rows0], g.at[2, rows0], g_ss.at[4], g_rs.at[4], at_y(1))]
    g_fwd[0].start()
    g_out[1].wait_recv()
    g_fwd.append(send(g.at[3, rows1], g.at[2, rows1], g_ss.at[5], g_rs.at[5], at_y(3)))
    g_fwd[1].start()

    w_out[0].wait_recv()
    rows = w_rows(lax.rem(x + 3, 4), 0)
    w_fwd = [send(wg.at[rows], wg.at[rows], w_ss.at[4], w_rs.at[4], at_x(1))]
    w_fwd[0].start()
    w_out[1].wait_recv()
    rows = w_rows(lax.rem(x + 1, 4), 1)
    w_fwd.append(send(wg.at[rows], wg.at[rows], w_ss.at[5], w_rs.at[5], at_x(3)))
    w_fwd[1].start()

    for cp in (g_out[2], g_out[3], g_fwd[0], g_fwd[1]):
        cp.wait_recv()
    proj_scale = D ** (-0.5)

    for cp in x_out:
        cp.wait_recv()
    gall = g[...].reshape(4 * T, C)
    for q in range(5):
        lhs = jnp.concatenate([xr[r, :, q * 256 : (q + 1) * 256] for r in range(4)], axis=0)
        pf[q * 256 : (q + 1) * 256, :] = (
            lax.dot_general(lhs, gall, (((0,), (0,)), ((), ())), preferred_element_type=F32)
            * proj_scale
        )

    def p_rows(d, half):
        return pf[pl.ds(pl.multiple_of(lax.rem(x + d, 4) * R + half * H, 32), H), :]

    s_opp[0:H, :] = p_rows(2, 0).astype(BF16)
    s_opp[H:R, :] = p_rows(2, 1).astype(BF16)
    p_out = [
        send(s_opp.at[pl.ds(0, H)], o_left, p_ss.at[0], p_rs.at[0], at_x(1)),
        send(s_opp.at[pl.ds(H, H)], o_right, p_ss.at[1], p_rs.at[1], at_x(3)),
    ]
    for cp in p_out:
        cp.start()
    s_right[H:R, :] = p_rows(1, 1).astype(BF16)
    s_left[0:H, :] = p_rows(3, 0).astype(BF16)
    p_out += [
        send(s_right.at[pl.ds(H, H)], r_left.at[pl.ds(H, H)], p_ss.at[2], p_rs.at[2], at_x(1)),
        send(s_left.at[pl.ds(0, H)], r_right.at[pl.ds(0, H)], p_ss.at[3], p_rs.at[3], at_x(3)),
    ]
    for cp in p_out[2:]:
        cp.start()
    p_out += [
        send(s_right.at[pl.ds(0, H)], r_left.at[pl.ds(0, H)], p_ss.at[4], p_rs.at[4], at_x(1)),
        send(s_left.at[pl.ds(H, H)], r_right.at[pl.ds(H, H)], p_ss.at[5], p_rs.at[5], at_x(3)),
    ]

    for cp in (w_out[2], w_out[3], w_fwd[0], w_fwd[1]):
        cp.wait_recv()

    sr_out = []

    def s_recv(i, n):
        rows = pl.ds(pl.multiple_of(i * MB, MB), MB)
        return send(ss.at[0, rows], sr.at[0, rows], s_ss.at[i, n], s_rs.at[i, n], at_y(1))

    for i in range(NMB):
        rows = pl.ds(i * MB, MB)
        lhs = jnp.concatenate([g[r, i * MB : (i + 1) * MB, :] for r in range(4)], axis=0)
        for q in range(5):
            cols = slice(q * 256, (q + 1) * 256)
            v = (
                lax.dot_general(
                    lhs, wg[q * 256 : (q + 1) * 256, :], (((1,), (1,)), ((), ())),
                    preferred_element_type=F32,
                )
                * proj_scale
            ).astype(BF16)
            for r in range(1, 4):
                ss[r, i * MB : (i + 1) * MB, cols] = v[r * MB : (r + 1) * MB]
            sr[y, i * MB : (i + 1) * MB, cols] = v[0:MB]
        for n, r in enumerate([2, 1, 3]):
            cp = send(ss.at[r, rows], sr.at[y, rows], s_ss.at[i, n], s_rs.at[i, n], at_y(4 - r))
            cp.start()
            sr_out.append(cp)

    def reduce_forward():
        p_out[0].wait_recv()
        s_right[0:H, :] = (p_rows(1, 0) + o_left[...].astype(F32)).astype(BF16)
        p_out[4].start()
        p_out[1].wait_recv()
        s_left[H:R, :] = (p_rows(3, 1) + o_right[...].astype(F32)).astype(BF16)
        p_out[5].start()

    mn_copy = pltpu.make_async_copy(mom, mn_hbm, out_sem.at[0])
    sn_copy = pltpu.make_async_copy(sec, sn_hbm, out_sem.at[1])
    ro_copy = pltpu.make_async_copy(ro, ro_hbm, out_sem.at[2])

    r_out = [
        send(
            rs.at[lax.rem(f + k, 16)], rr.at[f], r_ss.at[k - 1], r_rs.at[k - 1],
            (s, lax.rem(f + k, 16)),
        )
        for k in range(1, 16)
    ]

    def update():
        for cp in p_out[2:]:
            cp.wait_recv()
        loads[3].wait()
        loads[4].wait()

        def adam(k, carry):
            rows = pl.ds(pl.multiple_of(k * 32, 32), 32)
            grad = (
                pf[pl.ds(pl.multiple_of(x * R + k * 32, 32), 32), :]
                + r_left[rows, :].astype(F32)
                + r_right[rows, :].astype(F32)
            )
            m = beta_one * mom[rows, :] + (1.0 - beta_one) * grad
            v = beta_two * sec[rows, :] + (1.0 - beta_two) * grad * grad
            mom[rows, :] = m
            sec[rows, :] = v
            step = m * (1.0 / bias_one) / (jnp.sqrt(v * (1.0 / bias_two)) + adam_eps)
            old = mas[rows, :]
            wnew[rows, :] = (old - learn_rate * (step + weight_decay * old)).astype(BF16)
            return carry

        lax.fori_loop(0, R // 32, adam, 0)
        mn_copy.start()
        sn_copy.start()

        ia = lax.broadcasted_iota(jnp.int32, (128, 128), 0)
        ib = lax.broadcasted_iota(jnp.int32, (128, 128), 1)
        eye = jnp.where(ia == ib, 1.0, 0.0).astype(BF16)
        for j in range(4):
            o = owner[j]
            for p in range(2):
                v = wnew[:, p * 512 : p * 512 + 128]
                for h in range(1, 4):
                    v = jnp.where(o == h, wnew[:, p * 512 + h * 128 : p * 512 + (h + 1) * 128], v)
                t = lax.dot_general(
                    eye, v, (((1,), (1,)), ((), ())), preferred_element_type=F32
                ).astype(BF16)
                rs[j * 4 + p * 2] = t[0:RO]
                rs[j * 4 + p * 2 + 1] = t[RO : 2 * RO]
        for cp in r_out:
            cp.start()
        rr[f] = rs[f]

    def chain_rows(k):
        return pl.ds(pl.multiple_of(k * CH, CH), CH)

    def e_copy(k):
        rows = chain_rows(k)
        return send(es.at[:, rows], er.at[:, rows], e_ss.at[k], e_rs.at[k], partner)

    def hop(src, dst, sems, k, q, dev):
        rows = chain_rows(k)
        return send(src.at[q, rows], dst.at[q, rows], sems[0].at[k, q], sems[1].at[k, q], dev)

    def d_copy(k, q):
        return hop(ds, dr, (d_ss, d_rs), k, q, below)

    def l_copy(k, q):
        return hop(ls, lr, (l_ss, l_rs), k, q, below)

    def u_copy(k, q):
        return hop(us, ur, (u_ss, u_rs), k, q, above)

    def u_pass(k, q):
        return hop(ur, ur, (u_ss, u_rs), k, q, above)

    def m_copy(k, q):
        return hop(ms, mr, (m_ss, m_rs), k, q, partner)

    def og_copy(k):
        rows = chain_rows(k)
        return [
            pltpu.make_async_copy(
                out.at[b, rows], ig_hbm.at[rows, pl.ds(b * QD, QD)], og_sem.at[k, b]
            )
            for b in range(4)
        ]

    def pair_sum(k, q):
        rows = chain_rows(k)
        return own[c * 2 + q, rows, :] + er[q, rows, :].astype(F32)

    def own_step(k):
        rows = chain_rows(k)
        acc = jnp.zeros((CH, 1), F32)
        for b in range(4):
            t = tok[rows, b * QD : (b + 1) * QD].astype(F32)
            sc = sr[b, rows, :].astype(F32) * gain[:, b * QD : (b + 1) * QD]
            acc = acc + jnp.sum(sc * t, axis=-1, keepdims=True)
        iv = inv[rows, 0:1]
        coef = iv * iv * iv * (acc * (1.0 / D))
        for b in range(4):
            t = tok[rows, b * QD : (b + 1) * QD].astype(F32)
            sc = sr[b, rows, :].astype(F32) * gain[:, b * QD : (b + 1) * QD]
            own[b, rows, :] = iv * sc - t * coef
        for q in range(2):
            es[q, rows, :] = own[(1 - c) * 2 + q, rows, :].astype(BF16)
        e_copy(k).start()

    def when_step(t, lag, role, fn):
        k = t - lag

        @pl.when(role & (k >= 0) & (k < NCH))
        def _():
            fn(k)

    def down_step(k):
        rows = chain_rows(k)
        for q in range(2):

            @pl.when(z < 7)
            def _():
                d_copy(k, q).wait_recv()

            @pl.when(z > 2)
            def _():
                ds[q, rows, :] = (dr[q, rows, :].astype(F32) + pair_sum(k, q)).astype(BF16)
                d_copy(k, q).start()

    def low_step(k):
        rows = chain_rows(k)
        for q in range(2):

            @pl.when(z < 3)
            def _():
                l_copy(k, q).wait_recv()

            @pl.when(z > 0)
            def _():
                ls[q, rows, :] = (lr[q, rows, :].astype(F32) + pair_sum(k, q)).astype(BF16)
                l_copy(k, q).start()

    def up_step(k):
        rows = chain_rows(k)
        for q in range(2):

            @pl.when(z != 4)
            def _():
                u_copy(k, q).wait_recv()

            @pl.when(z >= 4)
            def _():
                us[q, rows, :] = (ur[q, rows, :].astype(F32) + pair_sum(k, q)).astype(BF16)
                u_copy(k, q).start()

            @pl.when(z == 0)
            def _():
                u_pass(k, q).start()

    def final_step(k):
        rows = chain_rows(k)

        def finish(q, u):
            b = c * 2 + q
            mine = u + own[b, rows, :]
            both = mine + er[q, rows, :].astype(F32)
            ms[q, rows, :] = jnp.where(c == 0, u, both).astype(BF16)
            m_copy(k, q).start()
            out[b, rows, :] = jnp.where(c == 0, both, mine).astype(BF16)

        for q in range(2):

            @pl.when(z >= 2)
            def _():
                finish(q, dr[q, rows, :].astype(F32))

            @pl.when(z < 2)
            def _():
                finish(q, ur[q, rows, :].astype(F32) + lr[q, rows, :].astype(F32))

    def other_step(k):
        rows = chain_rows(k)
        for q in range(2):
            m_copy(k, q).wait_recv()
            b = (1 - c) * 2 + q
            m = mr[q, rows, :].astype(F32)
            out[b, rows, :] = jnp.where(c == 1, m + own[b, rows, :], m).astype(BF16)
        for cp in og_copy(k):
            cp.start()

    up_lag = 1 + HOP * jnp.where(z >= 4, z - 4, 4 + z)
    down_lag = 1 + HOP * (7 - z)
    low_lag = 1 + HOP * (3 - z)
    final_lag = jnp.where(z >= 2, down_lag, up_lag)

    def slot(t, carry):
        @pl.when(t < NCH)
        def _():
            @pl.when(t % 2 == 0)
            def _():
                for n in range(3):
                    s_recv(t // 2, n).wait_recv()

            own_step(t)

        @pl.when((t >= 1) & (t <= NCH))
        def _():
            e_copy(t - 1).wait_recv()

        when_step(t, low_lag, z <= 3, low_step)
        when_step(t, up_lag, (z >= 4) | (z <= 1), up_step)
        when_step(t, down_lag, z >= 2, down_step)
        when_step(t, final_lag, z >= 0, final_step)
        when_step(t, final_lag + 1, z >= 0, other_step)

        @pl.when(t == FORWARD_SLOT)
        def _():
            reduce_forward()

        @pl.when(t == UPDATE_SLOT)
        def _():
            update()

        return carry

    lax.fori_loop(0, NCH + 2 + 5 * HOP, slot, 0)

    for cp in r_out:
        cp.wait_recv()
    for i in range(8):
        ro[:, i * 2 * R : (i + 1) * 2 * R] = jnp.concatenate([rr[2 * i], rr[2 * i + 1]], axis=1)
    ro_copy.start()

    for cp in w_out + w_fwd + g_out + g_fwd + x_out + sr_out + p_out + r_out:
        cp.wait_send()

    def drain(k, carry):
        e_copy(k).wait_send()
        for q in range(2):
            m_copy(k, q).wait_send()

            @pl.when(z > 2)
            def _():
                d_copy(k, q).wait_send()

            @pl.when((z > 0) & (z < 4))
            def _():
                l_copy(k, q).wait_send()

            @pl.when((z >= 4) | (z == 0))
            def _():
                u_copy(k, q).wait_send()

        for cp in og_copy(k):
            cp.wait()
        return carry

    lax.fori_loop(0, NCH, drain, 0)
    mn_copy.wait()
    sn_copy.wait()
    ro_copy.wait()


def land(*refs):
    srcs, dsts, bufs, (in_sem, out_sem) = refs[:4], refs[4:8], refs[8:12], refs[12:]
    ins, outs = [], []
    for i in range(4):
        rows = srcs[i].shape[0] // LAND
        for j in range(LAND):
            part = pl.ds(j * rows, rows)
            ins.append(pltpu.make_async_copy(srcs[i].at[part], bufs[i].at[part], in_sem.at[i, j]))
            outs.append(pltpu.make_async_copy(bufs[i].at[part], dsts[i].at[part], out_sem.at[i, j]))
    for cp in ins:
        cp.start()
    for cp, nxt in zip(ins, outs):
        cp.wait()
        nxt.start()
    for cp in outs:
        cp.wait()


def shards(tokens, cotangents, norm_gain, master, moment, second, head_owner, plan):
    hbm = pl.BlockSpec(memory_space=pl.ANY)
    vmem = pl.BlockSpec(memory_space=pltpu.VMEM)
    smem = pl.BlockSpec(memory_space=pltpu.SMEM)
    V = pltpu.VMEM
    dma = pltpu.SemaphoreType.DMA
    scratch = [
        V((T, D), BF16), V((T, C), BF16), V((R, C), F32), V((R, C), F32), V((R, C), F32),
        V((4 * R, C), BF16), V((4, T, C), BF16), V((4, T, QD), BF16), V((4, T, QD), BF16),
        V((4, T, QD), BF16), V((4, T, QD), BF16), V((T, 128), F32),
        V((4 * R, C), F32), V((R, C), BF16), V((R, C), BF16), V((R, C), BF16),
        V((H, C), BF16), V((H, C), BF16), V((R, C), BF16), V((R, C), BF16),
        V((R, C), BF16), V((16, RO, R), BF16), V((16, RO, R), BF16), V((RO, D), BF16),
        V((4, T, QD), F32), *[V((2, T, QD), BF16) for _ in range(10)], V((4, T, QD), BF16),
        dma((5,)), dma((3,)), dma((NCH, 4)),
        dma((6,)), dma((6,)), dma((6,)), dma((6,)), dma((3,)), dma((3,)),
        dma((NMB, 3)), dma((NMB, 3)), dma((6,)), dma((6,)), dma((15,)), dma((15,)),
        dma((NCH,)), dma((NCH,)), *[dma((NCH, 2)) for _ in range(8)],
    ]
    ig, mn, sn, ro = pl.pallas_call(
        kernel,
        out_shape=(
            jax.ShapeDtypeStruct((T, D), BF16),
            jax.ShapeDtypeStruct((R, C), F32),
            jax.ShapeDtypeStruct((R, C), F32),
            jax.ShapeDtypeStruct((RO, D), BF16),
        ),
        in_specs=[hbm, hbm, vmem, hbm, hbm, hbm, smem, smem],
        out_specs=(hbm, hbm, hbm, hbm),
        scratch_shapes=scratch,
        name="layer_backward",
        cost_estimate=pl.CostEstimate(
            flops=4 * T * C * D, bytes_accessed=12_000_000, transcendentals=2 * R * C
        ),
        compiler_params=pltpu.CompilerParams(
            collective_id=0, has_side_effects=True, vmem_limit_bytes=56 * 1024 * 1024
        ),
    )(tokens[0], cotangents[0], norm_gain, master[0], moment[0], second[0], head_owner[0], plan)
    outs = (ig, mn, sn, ro)
    outs = pl.pallas_call(
        land,
        out_shape=tuple(jax.ShapeDtypeStruct(v.shape, v.dtype) for v in outs),
        in_specs=[hbm] * 4,
        out_specs=(hbm,) * 4,
        scratch_shapes=[V(v.shape, v.dtype) for v in outs] + [dma((4, LAND)), dma((4, LAND))],
        name="land",
    )(*outs)
    return tuple(v[None] for v in outs)


def solution(mesh):
    in_specs = (
        P("section", "fsdp", None),
        P("section", "fsdp", None),
        P("section", None),
        P("section", "fsdp", None),
        P("section", "fsdp", None),
        P("section", "fsdp", None),
        P("section", None),
        P(),
    )
    out_specs = (
        P("section", "fsdp", None),
        P("section", "fsdp", None),
        P("section", "fsdp", None),
        P("section", "fsdp", None),
    )
    return jax.shard_map(shards, mesh=mesh, in_specs=in_specs, out_specs=out_specs, check_vma=False)
```

```python
import jax
import jax.numpy as jnp
from jax import lax
from jax.experimental import pallas as pl
from jax.experimental.pallas import tpu as pltpu
from jax.sharding import PartitionSpec as P

beta_one = 0.9
beta_two = 0.95
bias_one = 1.0 - 0.9**10
bias_two = 1.0 - 0.95**10
adam_eps = 1e-08
learn_rate = 0.02
weight_decay = 0.1
norm_eps = 1e-06

MESH = pl.DeviceIdType.MESH
F32 = jnp.float32
BF16 = jnp.bfloat16

D = 5120
C = 1024
T = 128
R = 320
H = R // 2
QD = D // 4
MB = 32
NMB = 4
CH = 16
NCH = T // CH
HOP = 2
FORWARD_SLOT = 4
UPDATE_SLOT = 11
UROWS = 160
HEADS = 2
DIRECT_SLOT = 2
ROLLOUT_SLOT = 20
OPPOSITE_AFTER = 1
REST_AFTER = 2
BASE = 2
BACK = 2
LAND = 1
RO = 64


def kernel(
    tok_hbm, cot_hbm, gain, mas_hbm, mom_hbm, sec_hbm, owner, plan,
    ig_hbm, mn_hbm, sn_hbm, ro_hbm,
    tok, cot, mas, mom, sec,
    wg, g, xs, xr, ss, sr, inv,
    pf, s_opp, s_right, s_left, o_left, o_right, r_left, r_right,
    wnew, rs, rr, ro,
    own, es, er, ds, dr, us, ur, ls, lr, ms, mr, out,
    in_sem, out_sem, og_sem,
    w_ss, w_rs, g_ss, g_rs, x_ss, x_rs, s_ss, s_rs, p_ss, p_rs, r_ss, r_rs,
    e_ss, e_rs, d_ss, d_rs, u_ss, u_rs, l_ss, l_rs, m_ss, m_rs,
):
    s = lax.axis_index("section")
    f = lax.axis_index("fsdp")
    z, c = s // 2, s % 2
    y, x = f // 4, f % 4

    def at_x(d):
        return (s, y * 4 + lax.rem(x + d, 4))

    def at_y(d):
        return (s, lax.rem(y + d, 4) * 4 + x)

    partner = (z * 2 + 1 - c, f)
    below = (lax.rem(z + 7, 8) * 2 + c, f)
    above = (lax.rem(z + 1, 8) * 2 + c, f)

    def send(src, dst, ssem, rsem, dev):
        return pltpu.make_async_remote_copy(
            src_ref=src, dst_ref=dst, send_sem=ssem, recv_sem=rsem, device_id=dev, device_id_type=MESH
        )

    loads = [
        pltpu.make_async_copy(a, b, in_sem.at[i])
        for i, (a, b) in enumerate(
            [(mas_hbm, mas), (cot_hbm, cot), (tok_hbm, tok), (mom_hbm, mom), (sec_hbm, sec)]
        )
    ]
    for ld in loads[:2]:
        ld.start()

    bar = pltpu.get_barrier_semaphore()
    for k in range(1, 16):
        pl.semaphore_signal(bar, inc=1, device_id=(s, lax.rem(f + k, 16)), device_id_type=MESH)
    for dev in (partner, below, above):
        pl.semaphore_signal(bar, inc=1, device_id=dev, device_id_type=MESH)

    for top, ref in ((7, dr), (4, ur), (3, lr)):

        @pl.when(z == top)
        def _():
            ref[...] = jnp.zeros_like(ref)

    for ld in loads[2:]:
        ld.start()

    def w_rows(block, half):
        return pl.ds(pl.multiple_of(block * R + half * H, 32), H)

    loads[0].wait()
    wg[pl.ds(pl.multiple_of(x * R, 32), R), :] = mas[...].astype(BF16)

    loads[1].wait()
    for i in range(NMB):
        p = plan[i]
        v = cot[0:MB, :]
        for j in range(1, NMB):
            v = jnp.where(p == j, cot[j * MB : (j + 1) * MB, :], v)
        g[0, i * MB : (i + 1) * MB, :] = v

    pl.semaphore_wait(bar, 18)

    w_out = []
    for n, (dev, half) in enumerate([(1, 0), (3, 1), (1, 1), (3, 0)]):
        rows = w_rows(x, half)
        w_out.append(send(wg.at[rows], wg.at[rows], w_ss.at[n], w_rs.at[n], at_x(dev)))
    for cp in w_out[:2]:
        cp.start()

    g_out = []
    hg = T // 2
    for n, (dev, half) in enumerate([(1, 0), (3, 1), (1, 1), (3, 0)]):
        rows = pl.ds(half * hg, hg)
        g_out.append(send(g.at[0, rows], g.at[dev, rows], g_ss.at[n], g_rs.at[n], at_y(dev)))
    for cp in g_out:
        cp.start()

    loads[2].wait()

    def norm_chunk(k, carry):
        rows = pl.ds(pl.multiple_of(k * CH, CH), CH)
        acc = jnp.zeros((CH, 1), F32)
        for b in range(4):
            v = tok[rows, b * QD : (b + 1) * QD].astype(F32)
            acc = acc + jnp.sum(v * v, axis=-1, keepdims=True)
        iv = lax.rsqrt(acc * (1.0 / D) + norm_eps)
        inv[rows, :] = jnp.broadcast_to(iv, (CH, 128))
        for b in range(4):
            v = tok[rows, b * QD : (b + 1) * QD].astype(F32)
            xs[b, rows, :] = (v * iv * gain[:, b * QD : (b + 1) * QD]).astype(BF16)
        return carry

    lax.fori_loop(0, NCH, norm_chunk, 0)

    x_out = []
    for n, dev in enumerate([2, 1, 3]):
        x_out.append(
            send(xs.at[lax.rem(y + dev, 4)], xr.at[dev], x_ss.at[n], x_rs.at[n], at_y(dev))
        )
    for cp in x_out:
        cp.start()
    xr[0] = xs[y]

    for first, second in zip(w_out[:2], w_out[2:]):
        first.wait_send()
        second.start()

    g_out[0].wait_recv()
    rows0, rows1 = pl.ds(0, hg), pl.ds(hg, hg)
    g_fwd = [send(g.at[1, rows0], g.at[2, rows0], g_ss.at[4], g_rs.at[4], at_y(1))]
    g_fwd[0].start()
    g_out[1].wait_recv()
    g_fwd.append(send(g.at[3, rows1], g.at[2, rows1], g_ss.at[5], g_rs.at[5], at_y(3)))
    g_fwd[1].start()

    w_out[0].wait_recv()
    rows = w_rows(lax.rem(x + 3, 4), 0)
    w_fwd = [send(wg.at[rows], wg.at[rows], w_ss.at[4], w_rs.at[4], at_x(1))]
    w_fwd[0].start()
    w_out[1].wait_recv()
    rows = w_rows(lax.rem(x + 1, 4), 1)
    w_fwd.append(send(wg.at[rows], wg.at[rows], w_ss.at[5], w_rs.at[5], at_x(3)))
    w_fwd[1].start()

    for cp in (g_out[2], g_out[3], g_fwd[0], g_fwd[1]):
        cp.wait_recv()
    proj_scale = D ** (-0.5)

    sr_out = []

    def s_recv(i, n):
        rows = pl.ds(pl.multiple_of(i * MB, MB), MB)
        return send(ss.at[0, rows], sr.at[0, rows], s_ss.at[i, n], s_rs.at[i, n], at_y(1))

    def spread_block(i):
        rows = pl.ds(i * MB, MB)
        lhs = jnp.concatenate([g[r, i * MB : (i + 1) * MB, :] for r in range(4)], axis=0)
        for q in range(5):
            cols = slice(q * 256, (q + 1) * 256)
            v = (
                lax.dot_general(
                    lhs, wg[q * 256 : (q + 1) * 256, :], (((1,), (1,)), ((), ())),
                    preferred_element_type=F32,
                )
                * proj_scale
            ).astype(BF16)
            for r in range(1, 4):
                ss[r, i * MB : (i + 1) * MB, cols] = v[r * MB : (r + 1) * MB]
            sr[y, i * MB : (i + 1) * MB, cols] = v[0:MB]
        for n, r in enumerate([2, 1, 3]):
            cp = send(ss.at[r, rows], sr.at[y, rows], s_ss.at[i, n], s_rs.at[i, n], at_y(4 - r))
            cp.start()
            sr_out.append(cp)

    def gradient_block(i):
        q = lax.rem(lax.rem(x + 2, 4) + i, 5)
        cols = pl.ds(pl.multiple_of(q * 256, 256), 256)
        lhs = jnp.concatenate([xr[r, :, cols] for r in range(4)], axis=0)
        pf[cols, :] = (
            lax.dot_general(
                lhs, g[...].reshape(4 * T, C), (((0,), (0,)), ((), ())),
                preferred_element_type=F32,
            )
            * proj_scale
        )

    def p_rows(d, half):
        return pf[pl.ds(pl.multiple_of(lax.rem(x + d, 4) * R + half * H, 32), H), :]

    p_out = [
        send(s_opp.at[pl.ds(0, H)], o_left, p_ss.at[0], p_rs.at[0], at_x(1)),
        send(s_opp.at[pl.ds(H, H)], o_right, p_ss.at[1], p_rs.at[1], at_x(3)),
        send(s_right.at[pl.ds(H, H)], r_left.at[pl.ds(H, H)], p_ss.at[2], p_rs.at[2], at_x(1)),
        send(s_left.at[pl.ds(0, H)], r_right.at[pl.ds(0, H)], p_ss.at[3], p_rs.at[3], at_x(3)),
        send(s_right.at[pl.ds(0, H)], r_left.at[pl.ds(0, H)], p_ss.at[4], p_rs.at[4], at_x(1)),
        send(s_left.at[pl.ds(H, H)], r_right.at[pl.ds(H, H)], p_ss.at[5], p_rs.at[5], at_x(3)),
    ]

    def gradient_opposite():
        for cp in x_out:
            cp.wait_recv()
        for i in range(2):
            gradient_block(i)
        s_opp[0:H, :] = p_rows(2, 0).astype(BF16)
        s_opp[H:R, :] = p_rows(2, 1).astype(BF16)
        for cp in p_out[:2]:
            cp.start()

    def gradient_rest():
        for i in range(2, 5):
            gradient_block(i)
        s_right[H:R, :] = p_rows(1, 1).astype(BF16)
        s_left[0:H, :] = p_rows(3, 0).astype(BF16)

    for cp in (w_out[2], w_out[3], w_fwd[0], w_fwd[1]):
        cp.wait_recv()
    for i in range(NMB):
        spread_block(i)
        if i == OPPOSITE_AFTER:
            gradient_opposite()
        if i == REST_AFTER:
            gradient_rest()

    def reduce_direct():
        for first, second in zip(p_out[:2], p_out[2:4]):
            first.wait_send()
            second.start()

    def reduce_forward():
        p_out[0].wait_recv()
        s_right[0:H, :] = (p_rows(1, 0) + o_left[...].astype(F32)).astype(BF16)
        p_out[4].start()
        p_out[1].wait_recv()
        s_left[H:R, :] = (p_rows(3, 1) + o_right[...].astype(F32)).astype(BF16)
        p_out[5].start()

    mn_copy = pltpu.make_async_copy(mom, mn_hbm, out_sem.at[0])
    sn_copy = pltpu.make_async_copy(sec, sn_hbm, out_sem.at[1])
    ro_copy = pltpu.make_async_copy(ro, ro_hbm, out_sem.at[2])

    def r_send(dest):
        return send(rs.at[dest], rr.at[f], r_ss.at[dest], r_rs.at[f], (s, dest))

    def r_recv(src):
        return send(rs.at[src], rr.at[src], r_ss.at[src], r_rs.at[src], (s, src))

    def update_wait():
        for cp in p_out[2:]:
            cp.wait_recv()
        loads[3].wait()
        loads[4].wait()

    def update_rows(u):
        def adam(k, carry):
            row = u * UROWS + k * 32
            rows = pl.ds(pl.multiple_of(row, 32), 32)
            grad = (
                pf[pl.ds(pl.multiple_of(x * R + row, 32), 32), :]
                + r_left[rows, :].astype(F32)
                + r_right[rows, :].astype(F32)
            )
            m = beta_one * mom[rows, :] + (1.0 - beta_one) * grad
            v = beta_two * sec[rows, :] + (1.0 - beta_two) * grad * grad
            mom[rows, :] = m
            sec[rows, :] = v
            step = m * (1.0 / bias_one) / (jnp.sqrt(v * (1.0 / bias_two)) + adam_eps)
            old = mas[rows, :]
            wnew[rows, :] = (old - learn_rate * (step + weight_decay * old)).astype(BF16)
            return carry

        lax.fori_loop(0, UROWS // 32, adam, 0)

    def rollout_head(j):
        ia = lax.broadcasted_iota(jnp.int32, (128, 128), 0)
        ib = lax.broadcasted_iota(jnp.int32, (128, 128), 1)
        eye = jnp.where(ia == ib, 1.0, 0.0).astype(BF16)
        o = owner[j]
        for p in range(2):
            v = wnew[:, p * 512 : p * 512 + 128]
            for h in range(1, 4):
                v = jnp.where(o == h, wnew[:, p * 512 + h * 128 : p * 512 + (h + 1) * 128], v)
            t = lax.dot_general(
                eye, v, (((1,), (1,)), ((), ())), preferred_element_type=F32
            ).astype(BF16)
            for half in range(2):
                dest = j * 4 + p * 2 + half
                rs[dest] = t[half * RO : (half + 1) * RO]

                @pl.when(dest != f)
                def _():
                    r_send(dest).start()

    def chain_rows(k):
        return pl.ds(pl.multiple_of(k * CH, CH), CH)

    def e_copy(k):
        rows = chain_rows(k)
        return send(es.at[:, rows], er.at[:, rows], e_ss.at[k], e_rs.at[k], partner)

    def hop(src, dst, sems, k, q, dev):
        rows = chain_rows(k)
        return send(src.at[q, rows], dst.at[q, rows], sems[0].at[k, q], sems[1].at[k, q], dev)

    def d_copy(k, q):
        return hop(ds, dr, (d_ss, d_rs), k, q, below)

    def l_copy(k, q):
        return hop(ls, lr, (l_ss, l_rs), k, q, below)

    def u_copy(k, q):
        return hop(us, ur, (u_ss, u_rs), k, q, above)

    def u_pass(k, q):
        return hop(ur, ur, (u_ss, u_rs), k, q, above)

    def m_copy(k):
        rows = pl.ds(pl.multiple_of((k // 2) * 2 * CH, 2 * CH), 2 * CH)
        return send(
            ms.at[:, rows], mr.at[:, rows], m_ss.at[k // 2], m_rs.at[k // 2], partner
        )

    def og_copy(k):
        rows = pl.ds(pl.multiple_of((k // 2) * 2 * CH, 2 * CH), 2 * CH)
        return pltpu.make_async_copy(out.at[rows], ig_hbm.at[rows], og_sem.at[k // 2])

    def quarter(b):
        return pl.ds(pl.multiple_of(b * QD, QD), QD)

    def pair_sum(k, q):
        rows = chain_rows(k)
        return own[c * 2 + q, rows, :] + er[q, rows, :].astype(F32)

    def own_step(k):
        rows = chain_rows(k)
        acc = jnp.zeros((CH, 1), F32)
        for b in range(4):
            t = tok[rows, b * QD : (b + 1) * QD].astype(F32)
            sc = sr[b, rows, :].astype(F32) * gain[:, b * QD : (b + 1) * QD]
            acc = acc + jnp.sum(sc * t, axis=-1, keepdims=True)
        iv = inv[rows, 0:1]
        coef = iv * iv * iv * (acc * (1.0 / D))
        for b in range(4):
            t = tok[rows, b * QD : (b + 1) * QD].astype(F32)
            sc = sr[b, rows, :].astype(F32) * gain[:, b * QD : (b + 1) * QD]
            own[b, rows, :] = iv * sc - t * coef
        for q in range(2):
            es[q, rows, :] = own[(1 - c) * 2 + q, rows, :].astype(BF16)
        e_copy(k).start()

    def when_step(t, lag, role, fn):
        k = t - lag

        @pl.when(role & (k >= 0) & (k < NCH))
        def _():
            fn(k)

    def down_step(k):
        rows = chain_rows(k)
        for q in range(2):

            @pl.when(z < 7)
            def _():
                d_copy(k, q).wait_recv()

            @pl.when(z > 2)
            def _():
                ds[q, rows, :] = (dr[q, rows, :].astype(F32) + pair_sum(k, q)).astype(BF16)
                d_copy(k, q).start()

    def low_step(k):
        rows = chain_rows(k)
        for q in range(2):

            @pl.when(z < 3)
            def _():
                l_copy(k, q).wait_recv()

            @pl.when(z > 0)
            def _():
                ls[q, rows, :] = (lr[q, rows, :].astype(F32) + pair_sum(k, q)).astype(BF16)
                l_copy(k, q).start()

    def up_step(k):
        rows = chain_rows(k)
        for q in range(2):

            @pl.when(z != 4)
            def _():
                u_copy(k, q).wait_recv()

            @pl.when(z >= 4)
            def _():
                us[q, rows, :] = (ur[q, rows, :].astype(F32) + pair_sum(k, q)).astype(BF16)
                u_copy(k, q).start()

            @pl.when(z == 0)
            def _():
                u_pass(k, q).start()

    def final_step(k):
        rows = chain_rows(k)

        def finish(q, u):
            b = c * 2 + q
            mine = u + own[b, rows, :]
            both = mine + er[q, rows, :].astype(F32)
            ms[q, rows, :] = jnp.where(c == 0, u, both).astype(BF16)
            out[rows, quarter(b)] = jnp.where(c == 0, both, mine).astype(BF16)

        @pl.when(z >= 2)
        def _():
            for q in range(2):
                finish(q, dr[q, rows, :].astype(F32))

        @pl.when(z < 2)
        def _():
            for q in range(2):
                finish(q, ur[q, rows, :].astype(F32) + lr[q, rows, :].astype(F32))

        @pl.when(k % 2 == 1)
        def _():
            m_copy(k).start()

    def other_step(k):
        @pl.when(k % 2 == 1)
        def _():
            rows = pl.ds(pl.multiple_of((k // 2) * 2 * CH, 2 * CH), 2 * CH)
            m_copy(k).wait_recv()
            for q in range(2):
                b = (1 - c) * 2 + q
                m = mr[q, rows, :].astype(F32)
                out[rows, quarter(b)] = jnp.where(c == 1, m + own[b, rows, :], m).astype(BF16)
            og_copy(k).start()

    up_lag = BASE + HOP * jnp.where(z >= 4, z - 4, 4 + z)
    down_lag = BASE + HOP * (7 - z)
    low_lag = BASE + HOP * (3 - z)
    final_lag = jnp.where(z >= 2, down_lag, up_lag)

    def slot(t, carry):
        @pl.when(t < NCH)
        def _():
            @pl.when(t % 2 == 0)
            def _():
                for n in range(3):
                    s_recv(t // 2, n).wait_recv()

            own_step(t)

        @pl.when((t >= BASE) & (t < NCH + BASE))
        def _():
            e_copy(t - BASE).wait_recv()

        when_step(t, low_lag, z <= 3, low_step)
        when_step(t, up_lag, (z >= 4) | (z <= 1), up_step)
        when_step(t, down_lag, z >= 2, down_step)
        when_step(t, final_lag, z >= 0, final_step)
        when_step(t, final_lag + BACK, z >= 0, other_step)

        @pl.when(t == DIRECT_SLOT)
        def _():
            reduce_direct()

        @pl.when(t == FORWARD_SLOT)
        def _():
            reduce_forward()

        u = t - UPDATE_SLOT

        @pl.when(u == 0)
        def _():
            update_wait()

        @pl.when((u >= 0) & (u < R // UROWS))
        def _():
            update_rows(u)

        @pl.when(u == R // UROWS)
        def _():
            mn_copy.start()
            sn_copy.start()

        j = u - R // UROWS

        @pl.when((j >= 0) & (j < 4 // HEADS))
        def _():
            for n in range(HEADS):
                rollout_head(j * HEADS + n)

        @pl.when(t == ROLLOUT_SLOT)
        def _():
            rr[f] = rs[f]
            for k in range(1, 16):
                r_recv(lax.rem(f + k, 16)).wait_recv()
            for i in range(8):
                ro[:, i * 2 * R : (i + 1) * 2 * R] = jnp.concatenate(
                    [rr[2 * i], rr[2 * i + 1]], axis=1
                )
            ro_copy.start()

        return carry

    lax.fori_loop(0, NCH + BASE + BACK + 5 * HOP, slot, 0)

    for cp in w_out[2:] + w_fwd + g_out + g_fwd + x_out + sr_out + p_out[2:]:
        cp.wait_send()
    for k in range(1, 16):
        r_send(lax.rem(f + k, 16)).wait_send()

    def drain(k, carry):
        e_copy(k).wait_send()

        @pl.when(k % 2 == 1)
        def _():
            m_copy(k).wait_send()
            og_copy(k).wait()

        for q in range(2):

            @pl.when(z > 2)
            def _():
                d_copy(k, q).wait_send()

            @pl.when((z > 0) & (z < 4))
            def _():
                l_copy(k, q).wait_send()

            @pl.when((z >= 4) | (z == 0))
            def _():
                u_copy(k, q).wait_send()

        return carry

    lax.fori_loop(0, NCH, drain, 0)
    mn_copy.wait()
    sn_copy.wait()
    ro_copy.wait()


def land(*refs):
    srcs, dsts, bufs, (in_sem, out_sem) = refs[:4], refs[4:8], refs[8:12], refs[12:]
    ins, outs = [], []
    for i in range(4):
        rows = srcs[i].shape[0] // LAND
        for j in range(LAND):
            part = pl.ds(j * rows, rows)
            ins.append(pltpu.make_async_copy(srcs[i].at[part], bufs[i].at[part], in_sem.at[i, j]))
            outs.append(pltpu.make_async_copy(bufs[i].at[part], dsts[i].at[part], out_sem.at[i, j]))
    for cp in ins:
        cp.start()
    for cp, nxt in zip(ins, outs):
        cp.wait()
        nxt.start()
    for cp in outs:
        cp.wait()


def shards(tokens, cotangents, norm_gain, master, moment, second, head_owner, plan):
    hbm = pl.BlockSpec(memory_space=pl.ANY)
    vmem = pl.BlockSpec(memory_space=pltpu.VMEM)
    smem = pl.BlockSpec(memory_space=pltpu.SMEM)
    V = pltpu.VMEM
    dma = pltpu.SemaphoreType.DMA
    scratch = [
        V((T, D), BF16), V((T, C), BF16), V((R, C), F32), V((R, C), F32), V((R, C), F32),
        V((4 * R, C), BF16), V((4, T, C), BF16), V((4, T, QD), BF16), V((4, T, QD), BF16),
        V((4, T, QD), BF16), V((4, T, QD), BF16), V((T, 128), F32),
        V((4 * R, C), F32), V((R, C), BF16), V((R, C), BF16), V((R, C), BF16),
        V((H, C), BF16), V((H, C), BF16), V((R, C), BF16), V((R, C), BF16),
        V((R, C), BF16), V((16, RO, R), BF16), V((16, RO, R), BF16), V((RO, D), BF16),
        V((4, T, QD), F32), *[V((2, T, QD), BF16) for _ in range(10)], V((T, D), BF16),
        dma((5,)), dma((3,)), dma((NCH,)),
        dma((6,)), dma((6,)), dma((6,)), dma((6,)), dma((3,)), dma((3,)),
        dma((NMB, 3)), dma((NMB, 3)), dma((6,)), dma((6,)), dma((16,)), dma((16,)),
        dma((NCH,)), dma((NCH,)), *[dma((NCH, 2)) for _ in range(6)],
        dma((NCH,)), dma((NCH,)),
    ]
    ig, mn, sn, ro = pl.pallas_call(
        kernel,
        out_shape=(
            jax.ShapeDtypeStruct((T, D), BF16),
            jax.ShapeDtypeStruct((R, C), F32),
            jax.ShapeDtypeStruct((R, C), F32),
            jax.ShapeDtypeStruct((RO, D), BF16),
        ),
        in_specs=[hbm, hbm, vmem, hbm, hbm, hbm, smem, smem],
        out_specs=(hbm, hbm, hbm, hbm),
        scratch_shapes=scratch,
        name="layer_backward",
        cost_estimate=pl.CostEstimate(
            flops=4 * T * C * D, bytes_accessed=12_000_000, transcendentals=2 * R * C
        ),
        compiler_params=pltpu.CompilerParams(
            collective_id=0, has_side_effects=True, vmem_limit_bytes=56 * 1024 * 1024
        ),
    )(tokens[0], cotangents[0], norm_gain, master[0], moment[0], second[0], head_owner[0], plan)
    outs = (ig, mn, sn, ro)
    outs = pl.pallas_call(
        land,
        out_shape=tuple(jax.ShapeDtypeStruct(v.shape, v.dtype) for v in outs),
        in_specs=[hbm] * 4,
        out_specs=(hbm,) * 4,
        scratch_shapes=[V(v.shape, v.dtype) for v in outs] + [dma((4, LAND)), dma((4, LAND))],
        name="land",
    )(*outs)
    return tuple(v[None] for v in outs)


def solution(mesh):
    in_specs = (
        P("section", "fsdp", None),
        P("section", "fsdp", None),
        P("section", None),
        P("section", "fsdp", None),
        P("section", "fsdp", None),
        P("section", "fsdp", None),
        P("section", None),
        P(),
    )
    out_specs = (
        P("section", "fsdp", None),
        P("section", "fsdp", None),
        P("section", "fsdp", None),
        P("section", "fsdp", None),
    )
    return jax.shard_map(shards, mesh=mesh, in_specs=in_specs, out_specs=out_specs, check_vma=False)
```

```python
import jax
import jax.numpy as jnp
from jax import lax
from jax.experimental import pallas as pl
from jax.experimental.pallas import tpu as pltpu
from jax.sharding import PartitionSpec as P

beta_one = 0.9
beta_two = 0.95
bias_one = 1.0 - 0.9**10
bias_two = 1.0 - 0.95**10
adam_eps = 1e-08
learn_rate = 0.02
weight_decay = 0.1
norm_eps = 1e-06

MESH = pl.DeviceIdType.MESH
F32 = jnp.float32
BF16 = jnp.bfloat16

D = 5120
C = 1024
T = 128
R = 320
H = R // 2
QD = D // 4
MB = 32
NMB = 4
CH = 16
NCH = T // CH
HOP = 2
FORWARD_SLOT = 4
UPDATE_SLOT = 11
UROWS = 160
HEADS = 2
DIRECT_SLOT = 2
ROLLOUT_SLOT = 20
BASE = 2
BACK = 2
LAND = 1
RO = 64


def kernel(
    tok_hbm, cot_hbm, gain, mas_hbm, mom_hbm, sec_hbm, owner, plan,
    ig_hbm, mn_hbm, sn_hbm, ro_hbm,
    tok, cot, mas, mom, sec,
    wg, g, xs, xr, ss, sr, inv,
    pf, s_opp, s_right, s_left, o_left, o_right, r_left, r_right,
    wnew, rs, rr, ro,
    own, es, er, ds, dr, us, ur, ls, lr, ms, mr, out,
    in_sem, out_sem, og_sem,
    w_ss, w_rs, g_ss, g_rs, x_ss, x_rs, s_ss, s_rs, p_ss, p_rs, r_ss, r_rs,
    e_ss, e_rs, d_ss, d_rs, u_ss, u_rs, l_ss, l_rs, m_ss, m_rs,
):
    s = lax.axis_index("section")
    f = lax.axis_index("fsdp")
    z, c = s // 2, s % 2
    y, x = f // 4, f % 4

    def at_x(d):
        return (s, y * 4 + lax.rem(x + d, 4))

    def at_y(d):
        return (s, lax.rem(y + d, 4) * 4 + x)

    partner = (z * 2 + 1 - c, f)
    below = (lax.rem(z + 7, 8) * 2 + c, f)
    above = (lax.rem(z + 1, 8) * 2 + c, f)

    def send(src, dst, ssem, rsem, dev):
        return pltpu.make_async_remote_copy(
            src_ref=src, dst_ref=dst, send_sem=ssem, recv_sem=rsem, device_id=dev, device_id_type=MESH
        )

    loads = [
        pltpu.make_async_copy(a, b, in_sem.at[i])
        for i, (a, b) in enumerate(
            [(mas_hbm, mas), (cot_hbm, cot), (tok_hbm, tok), (mom_hbm, mom), (sec_hbm, sec)]
        )
    ]
    for ld in loads[:2]:
        ld.start()

    bar = pltpu.get_barrier_semaphore()
    for k in range(1, 16):
        pl.semaphore_signal(bar, inc=1, device_id=(s, lax.rem(f + k, 16)), device_id_type=MESH)
    for dev in (partner, below, above):
        pl.semaphore_signal(bar, inc=1, device_id=dev, device_id_type=MESH)

    for top, ref in ((7, dr), (4, ur), (3, lr)):

        @pl.when(z == top)
        def _():
            ref[...] = jnp.zeros_like(ref)

    for ld in loads[2:]:
        ld.start()

    def w_rows(block, half):
        return pl.ds(pl.multiple_of(block * R + half * H, 32), H)

    loads[0].wait()
    wg[pl.ds(pl.multiple_of(x * R, 32), R), :] = mas[...].astype(BF16)

    loads[1].wait()
    for i in range(NMB):
        p = plan[i]
        v = cot[0:MB, :]
        for j in range(1, NMB):
            v = jnp.where(p == j, cot[j * MB : (j + 1) * MB, :], v)
        g[0, i * MB : (i + 1) * MB, :] = v

    pl.semaphore_wait(bar, 18)

    w_out = []
    for n, (dev, half) in enumerate([(1, 0), (3, 1), (1, 1), (3, 0)]):
        rows = w_rows(x, half)
        w_out.append(send(wg.at[rows], wg.at[rows], w_ss.at[n], w_rs.at[n], at_x(dev)))
    for cp in w_out[:2]:
        cp.start()

    g_out = []
    hg = T // 2
    for n, (dev, half) in enumerate([(1, 0), (3, 1), (1, 1), (3, 0)]):
        rows = pl.ds(half * hg, hg)
        g_out.append(send(g.at[0, rows], g.at[dev, rows], g_ss.at[n], g_rs.at[n], at_y(dev)))
    for cp in g_out:
        cp.start()

    loads[2].wait()

    def norm_chunk(k, carry):
        rows = pl.ds(pl.multiple_of(k * CH, CH), CH)
        acc = jnp.zeros((CH, 1), F32)
        for b in range(4):
            v = tok[rows, b * QD : (b + 1) * QD].astype(F32)
            acc = acc + jnp.sum(v * v, axis=-1, keepdims=True)
        iv = lax.rsqrt(acc * (1.0 / D) + norm_eps)
        inv[rows, :] = jnp.broadcast_to(iv, (CH, 128))
        for b in range(4):
            v = tok[rows, b * QD : (b + 1) * QD].astype(F32)
            xs[b, rows, :] = (v * iv * gain[:, b * QD : (b + 1) * QD]).astype(BF16)
        return carry

    lax.fori_loop(0, NCH, norm_chunk, 0)

    x_out = []
    for n, dev in enumerate([2, 1, 3]):
        x_out.append(
            send(xs.at[lax.rem(y + dev, 4)], xr.at[dev], x_ss.at[n], x_rs.at[n], at_y(dev))
        )
    for cp in x_out:
        cp.start()
    xr[0] = xs[y]

    for first, second in zip(w_out[:2], w_out[2:]):
        first.wait_send()
        second.start()

    g_out[0].wait_recv()
    rows0, rows1 = pl.ds(0, hg), pl.ds(hg, hg)
    g_fwd = [send(g.at[1, rows0], g.at[2, rows0], g_ss.at[4], g_rs.at[4], at_y(1))]
    g_fwd[0].start()
    g_out[1].wait_recv()
    g_fwd.append(send(g.at[3, rows1], g.at[2, rows1], g_ss.at[5], g_rs.at[5], at_y(3)))
    g_fwd[1].start()

    w_out[0].wait_recv()
    rows = w_rows(lax.rem(x + 3, 4), 0)
    w_fwd = [send(wg.at[rows], wg.at[rows], w_ss.at[4], w_rs.at[4], at_x(1))]
    w_fwd[0].start()
    w_out[1].wait_recv()
    rows = w_rows(lax.rem(x + 1, 4), 1)
    w_fwd.append(send(wg.at[rows], wg.at[rows], w_ss.at[5], w_rs.at[5], at_x(3)))
    w_fwd[1].start()

    for cp in (g_out[2], g_out[3], g_fwd[0], g_fwd[1]):
        cp.wait_recv()
    proj_scale = D ** (-0.5)

    sr_out = []

    def s_recv(i, n):
        rows = pl.ds(pl.multiple_of(i * MB, MB), MB)
        return send(ss.at[0, rows], sr.at[0, rows], s_ss.at[i, n], s_rs.at[i, n], at_y(1))

    def spread_pair(i):
        first = i * 2 * MB
        lhs = jnp.concatenate([g[r, first : first + 2 * MB, :] for r in range(4)], axis=0)
        for q in range(5):
            cols = slice(q * 256, (q + 1) * 256)
            v = (
                lax.dot_general(
                    lhs, wg[q * 256 : (q + 1) * 256, :], (((1,), (1,)), ((), ())),
                    preferred_element_type=F32,
                )
                * proj_scale
            ).astype(BF16)
            for r in range(1, 4):
                ss[r, first : first + 2 * MB, cols] = v[r * 2 * MB : (r + 1) * 2 * MB]
            sr[y, first : first + 2 * MB, cols] = v[0 : 2 * MB]
        for m in (2 * i, 2 * i + 1):
            rows = pl.ds(m * MB, MB)
            for n, r in enumerate([2, 1, 3]):
                cp = send(
                    ss.at[r, rows], sr.at[y, rows], s_ss.at[m, n], s_rs.at[m, n], at_y(4 - r)
                )
                cp.start()
                sr_out.append(cp)

    def gradient_block(i):
        q = lax.rem(lax.rem(x + 2, 4) + i, 5)
        cols = pl.ds(pl.multiple_of(q * 256, 256), 256)
        lhs = jnp.concatenate([xr[r, :, cols] for r in range(4)], axis=0)
        pf[cols, :] = (
            lax.dot_general(
                lhs, g[...].reshape(4 * T, C), (((0,), (0,)), ((), ())),
                preferred_element_type=F32,
            )
            * proj_scale
        )

    def p_rows(d, half):
        return pf[pl.ds(pl.multiple_of(lax.rem(x + d, 4) * R + half * H, 32), H), :]

    p_out = [
        send(s_opp.at[pl.ds(0, H)], o_left, p_ss.at[0], p_rs.at[0], at_x(1)),
        send(s_opp.at[pl.ds(H, H)], o_right, p_ss.at[1], p_rs.at[1], at_x(3)),
        send(s_right.at[pl.ds(H, H)], r_left.at[pl.ds(H, H)], p_ss.at[2], p_rs.at[2], at_x(1)),
        send(s_left.at[pl.ds(0, H)], r_right.at[pl.ds(0, H)], p_ss.at[3], p_rs.at[3], at_x(3)),
        send(s_right.at[pl.ds(0, H)], r_left.at[pl.ds(0, H)], p_ss.at[4], p_rs.at[4], at_x(1)),
        send(s_left.at[pl.ds(H, H)], r_right.at[pl.ds(H, H)], p_ss.at[5], p_rs.at[5], at_x(3)),
    ]

    def gradient_opposite():
        for cp in x_out:
            cp.wait_recv()
        for i in range(2):
            gradient_block(i)
        s_opp[0:H, :] = p_rows(2, 0).astype(BF16)
        s_opp[H:R, :] = p_rows(2, 1).astype(BF16)
        for cp in p_out[:2]:
            cp.start()

    def gradient_rest():
        for i in range(2, 5):
            gradient_block(i)
        s_right[H:R, :] = p_rows(1, 1).astype(BF16)
        s_left[0:H, :] = p_rows(3, 0).astype(BF16)

    for cp in (w_out[2], w_out[3], w_fwd[0], w_fwd[1]):
        cp.wait_recv()
    spread_pair(0)
    gradient_opposite()
    spread_pair(1)
    gradient_rest()

    def reduce_direct():
        for first, second in zip(p_out[:2], p_out[2:4]):
            first.wait_send()
            second.start()

    def reduce_forward():
        p_out[0].wait_recv()
        s_right[0:H, :] = (p_rows(1, 0) + o_left[...].astype(F32)).astype(BF16)
        p_out[4].start()
        p_out[1].wait_recv()
        s_left[H:R, :] = (p_rows(3, 1) + o_right[...].astype(F32)).astype(BF16)
        p_out[5].start()

    mn_copy = pltpu.make_async_copy(mom, mn_hbm, out_sem.at[0])
    sn_copy = pltpu.make_async_copy(sec, sn_hbm, out_sem.at[1])
    ro_copy = pltpu.make_async_copy(ro, ro_hbm, out_sem.at[2])

    def r_send(dest):
        return send(rs.at[dest], rr.at[f], r_ss.at[dest], r_rs.at[f], (s, dest))

    def r_recv(src):
        return send(rs.at[src], rr.at[src], r_ss.at[src], r_rs.at[src], (s, src))

    def update_wait():
        for cp in p_out[2:]:
            cp.wait_recv()
        loads[3].wait()
        loads[4].wait()

    def update_rows(u):
        def adam(k, carry):
            row = u * UROWS + k * 32
            rows = pl.ds(pl.multiple_of(row, 32), 32)
            grad = (
                pf[pl.ds(pl.multiple_of(x * R + row, 32), 32), :]
                + r_left[rows, :].astype(F32)
                + r_right[rows, :].astype(F32)
            )
            m = beta_one * mom[rows, :] + (1.0 - beta_one) * grad
            v = beta_two * sec[rows, :] + (1.0 - beta_two) * grad * grad
            mom[rows, :] = m
            sec[rows, :] = v
            step = m * (1.0 / bias_one) / (jnp.sqrt(v * (1.0 / bias_two)) + adam_eps)
            old = mas[rows, :]
            wnew[rows, :] = (old - learn_rate * (step + weight_decay * old)).astype(BF16)
            return carry

        lax.fori_loop(0, UROWS // 32, adam, 0)

    def rollout_head(j):
        ia = lax.broadcasted_iota(jnp.int32, (128, 128), 0)
        ib = lax.broadcasted_iota(jnp.int32, (128, 128), 1)
        eye = jnp.where(ia == ib, 1.0, 0.0).astype(BF16)
        o = owner[j]
        for p in range(2):
            v = wnew[:, p * 512 : p * 512 + 128]
            for h in range(1, 4):
                v = jnp.where(o == h, wnew[:, p * 512 + h * 128 : p * 512 + (h + 1) * 128], v)
            t = lax.dot_general(
                eye, v, (((1,), (1,)), ((), ())), preferred_element_type=F32
            ).astype(BF16)
            for half in range(2):
                dest = j * 4 + p * 2 + half
                rs[dest] = t[half * RO : (half + 1) * RO]

                @pl.when(dest != f)
                def _():
                    r_send(dest).start()

    def chain_rows(k):
        return pl.ds(pl.multiple_of(k * CH, CH), CH)

    def e_copy(k):
        rows = chain_rows(k)
        return send(es.at[:, rows], er.at[:, rows], e_ss.at[k], e_rs.at[k], partner)

    def hop(src, dst, sems, k, q, dev):
        rows = chain_rows(k)
        return send(src.at[q, rows], dst.at[q, rows], sems[0].at[k, q], sems[1].at[k, q], dev)

    def d_copy(k, q):
        return hop(ds, dr, (d_ss, d_rs), k, q, below)

    def l_copy(k, q):
        return hop(ls, lr, (l_ss, l_rs), k, q, below)

    def u_copy(k, q):
        return hop(us, ur, (u_ss, u_rs), k, q, above)

    def u_pass(k, q):
        return hop(ur, ur, (u_ss, u_rs), k, q, above)

    def m_copy(k):
        rows = pl.ds(pl.multiple_of((k // 2) * 2 * CH, 2 * CH), 2 * CH)
        return send(
            ms.at[:, rows], mr.at[:, rows], m_ss.at[k // 2], m_rs.at[k // 2], partner
        )

    def og_copy(k):
        rows = pl.ds(pl.multiple_of((k // 2) * 2 * CH, 2 * CH), 2 * CH)
        return pltpu.make_async_copy(out.at[rows], ig_hbm.at[rows], og_sem.at[k // 2])

    def quarter(b):
        return pl.ds(pl.multiple_of(b * QD, QD), QD)

    def pair_sum(k, q):
        rows = chain_rows(k)
        return own[c * 2 + q, rows, :] + er[q, rows, :].astype(F32)

    def own_step(k):
        rows = chain_rows(k)
        acc = jnp.zeros((CH, 1), F32)
        for b in range(4):
            t = tok[rows, b * QD : (b + 1) * QD].astype(F32)
            sc = sr[b, rows, :].astype(F32) * gain[:, b * QD : (b + 1) * QD]
            acc = acc + jnp.sum(sc * t, axis=-1, keepdims=True)
        iv = inv[rows, 0:1]
        coef = iv * iv * iv * (acc * (1.0 / D))
        for b in range(4):
            t = tok[rows, b * QD : (b + 1) * QD].astype(F32)
            sc = sr[b, rows, :].astype(F32) * gain[:, b * QD : (b + 1) * QD]
            own[b, rows, :] = iv * sc - t * coef
        for q in range(2):
            es[q, rows, :] = own[(1 - c) * 2 + q, rows, :].astype(BF16)
        e_copy(k).start()

    def when_step(t, lag, role, fn):
        k = t - lag

        @pl.when(role & (k >= 0) & (k < NCH))
        def _():
            fn(k)

    def down_step(k):
        rows = chain_rows(k)
        for q in range(2):

            @pl.when(z < 7)
            def _():
                d_copy(k, q).wait_recv()

            @pl.when(z > 2)
            def _():
                ds[q, rows, :] = (dr[q, rows, :].astype(F32) + pair_sum(k, q)).astype(BF16)
                d_copy(k, q).start()

    def low_step(k):
        rows = chain_rows(k)
        for q in range(2):

            @pl.when(z < 3)
            def _():
                l_copy(k, q).wait_recv()

            @pl.when(z > 0)
            def _():
                ls[q, rows, :] = (lr[q, rows, :].astype(F32) + pair_sum(k, q)).astype(BF16)
                l_copy(k, q).start()

    def up_step(k):
        rows = chain_rows(k)
        for q in range(2):

            @pl.when(z != 4)
            def _():
                u_copy(k, q).wait_recv()

            @pl.when(z >= 4)
            def _():
                us[q, rows, :] = (ur[q, rows, :].astype(F32) + pair_sum(k, q)).astype(BF16)
                u_copy(k, q).start()

            @pl.when(z == 0)
            def _():
                u_pass(k, q).start()

    def final_step(k):
        rows = chain_rows(k)

        def finish(q, u):
            b = c * 2 + q
            mine = u + own[b, rows, :]
            both = mine + er[q, rows, :].astype(F32)
            ms[q, rows, :] = jnp.where(c == 0, u, both).astype(BF16)
            out[rows, quarter(b)] = jnp.where(c == 0, both, mine).astype(BF16)

        @pl.when(z >= 2)
        def _():
            for q in range(2):
                finish(q, dr[q, rows, :].astype(F32))

        @pl.when(z < 2)
        def _():
            for q in range(2):
                finish(q, ur[q, rows, :].astype(F32) + lr[q, rows, :].astype(F32))

        @pl.when(k % 2 == 1)
        def _():
            m_copy(k).start()

    def other_step(k):
        @pl.when(k % 2 == 1)
        def _():
            rows = pl.ds(pl.multiple_of((k // 2) * 2 * CH, 2 * CH), 2 * CH)
            m_copy(k).wait_recv()
            for q in range(2):
                b = (1 - c) * 2 + q
                m = mr[q, rows, :].astype(F32)
                out[rows, quarter(b)] = jnp.where(c == 1, m + own[b, rows, :], m).astype(BF16)
            og_copy(k).start()

    up_lag = BASE + HOP * jnp.where(z >= 4, z - 4, 4 + z)
    down_lag = BASE + HOP * (7 - z)
    low_lag = BASE + HOP * (3 - z)
    final_lag = jnp.where(z >= 2, down_lag, up_lag)

    def slot(t, carry):
        @pl.when(t < NCH)
        def _():
            @pl.when(t % 2 == 0)
            def _():
                for n in range(3):
                    s_recv(t // 2, n).wait_recv()

            own_step(t)

        @pl.when((t >= BASE) & (t < NCH + BASE))
        def _():
            e_copy(t - BASE).wait_recv()

        when_step(t, low_lag, z <= 3, low_step)
        when_step(t, up_lag, (z >= 4) | (z <= 1), up_step)
        when_step(t, down_lag, z >= 2, down_step)
        when_step(t, final_lag, z >= 0, final_step)
        when_step(t, final_lag + BACK, z >= 0, other_step)

        @pl.when(t == DIRECT_SLOT)
        def _():
            reduce_direct()

        @pl.when(t == FORWARD_SLOT)
        def _():
            reduce_forward()

        u = t - UPDATE_SLOT

        @pl.when(u == 0)
        def _():
            update_wait()

        @pl.when((u >= 0) & (u < R // UROWS))
        def _():
            update_rows(u)

        @pl.when(u == R // UROWS)
        def _():
            mn_copy.start()
            sn_copy.start()

        j = u - R // UROWS

        @pl.when((j >= 0) & (j < 4 // HEADS))
        def _():
            for n in range(HEADS):
                rollout_head(j * HEADS + n)

        @pl.when(t == ROLLOUT_SLOT)
        def _():
            rr[f] = rs[f]
            for k in range(1, 16):
                r_recv(lax.rem(f + k, 16)).wait_recv()
            for i in range(8):
                ro[:, i * 2 * R : (i + 1) * 2 * R] = jnp.concatenate(
                    [rr[2 * i], rr[2 * i + 1]], axis=1
                )
            ro_copy.start()

        return carry

    lax.fori_loop(0, NCH + BASE + BACK + 5 * HOP, slot, 0)

    for cp in w_out[2:] + w_fwd + g_out + g_fwd + x_out + sr_out + p_out[2:]:
        cp.wait_send()
    for k in range(1, 16):
        r_send(lax.rem(f + k, 16)).wait_send()

    def drain(k, carry):
        e_copy(k).wait_send()

        @pl.when(k % 2 == 1)
        def _():
            m_copy(k).wait_send()
            og_copy(k).wait()

        for q in range(2):

            @pl.when(z > 2)
            def _():
                d_copy(k, q).wait_send()

            @pl.when((z > 0) & (z < 4))
            def _():
                l_copy(k, q).wait_send()

            @pl.when((z >= 4) | (z == 0))
            def _():
                u_copy(k, q).wait_send()

        return carry

    lax.fori_loop(0, NCH, drain, 0)
    mn_copy.wait()
    sn_copy.wait()
    ro_copy.wait()


def land(*refs):
    srcs, dsts, bufs, (in_sem, out_sem) = refs[:4], refs[4:8], refs[8:12], refs[12:]
    ins, outs = [], []
    for i in range(4):
        rows = srcs[i].shape[0] // LAND
        for j in range(LAND):
            part = pl.ds(j * rows, rows)
            ins.append(pltpu.make_async_copy(srcs[i].at[part], bufs[i].at[part], in_sem.at[i, j]))
            outs.append(pltpu.make_async_copy(bufs[i].at[part], dsts[i].at[part], out_sem.at[i, j]))
    for cp in ins:
        cp.start()
    for cp, nxt in zip(ins, outs):
        cp.wait()
        nxt.start()
    for cp in outs:
        cp.wait()


def shards(tokens, cotangents, norm_gain, master, moment, second, head_owner, plan):
    hbm = pl.BlockSpec(memory_space=pl.ANY)
    vmem = pl.BlockSpec(memory_space=pltpu.VMEM)
    smem = pl.BlockSpec(memory_space=pltpu.SMEM)
    V = pltpu.VMEM
    dma = pltpu.SemaphoreType.DMA
    scratch = [
        V((T, D), BF16), V((T, C), BF16), V((R, C), F32), V((R, C), F32), V((R, C), F32),
        V((4 * R, C), BF16), V((4, T, C), BF16), V((4, T, QD), BF16), V((4, T, QD), BF16),
        V((4, T, QD), BF16), V((4, T, QD), BF16), V((T, 128), F32),
        V((4 * R, C), F32), V((R, C), BF16), V((R, C), BF16), V((R, C), BF16),
        V((H, C), BF16), V((H, C), BF16), V((R, C), BF16), V((R, C), BF16),
        V((R, C), BF16), V((16, RO, R), BF16), V((16, RO, R), BF16), V((RO, D), BF16),
        V((4, T, QD), F32), *[V((2, T, QD), BF16) for _ in range(10)], V((T, D), BF16),
        dma((5,)), dma((3,)), dma((NCH,)),
        dma((6,)), dma((6,)), dma((6,)), dma((6,)), dma((3,)), dma((3,)),
        dma((NMB, 3)), dma((NMB, 3)), dma((6,)), dma((6,)), dma((16,)), dma((16,)),
        dma((NCH,)), dma((NCH,)), *[dma((NCH, 2)) for _ in range(6)],
        dma((NCH,)), dma((NCH,)),
    ]
    ig, mn, sn, ro = pl.pallas_call(
        kernel,
        out_shape=(
            jax.ShapeDtypeStruct((T, D), BF16),
            jax.ShapeDtypeStruct((R, C), F32),
            jax.ShapeDtypeStruct((R, C), F32),
            jax.ShapeDtypeStruct((RO, D), BF16),
        ),
        in_specs=[hbm, hbm, vmem, hbm, hbm, hbm, smem, smem],
        out_specs=(hbm, hbm, hbm, hbm),
        scratch_shapes=scratch,
        name="layer_backward",
        cost_estimate=pl.CostEstimate(
            flops=4 * T * C * D, bytes_accessed=12_000_000, transcendentals=2 * R * C
        ),
        compiler_params=pltpu.CompilerParams(
            collective_id=0, has_side_effects=True, vmem_limit_bytes=56 * 1024 * 1024
        ),
    )(tokens[0], cotangents[0], norm_gain, master[0], moment[0], second[0], head_owner[0], plan)
    outs = (ig, mn, sn, ro)
    outs = pl.pallas_call(
        land,
        out_shape=tuple(jax.ShapeDtypeStruct(v.shape, v.dtype) for v in outs),
        in_specs=[hbm] * 4,
        out_specs=(hbm,) * 4,
        scratch_shapes=[V(v.shape, v.dtype) for v in outs] + [dma((4, LAND)), dma((4, LAND))],
        name="land",
    )(*outs)
    return tuple(v[None] for v in outs)


def solution(mesh):
    in_specs = (
        P("section", "fsdp", None),
        P("section", "fsdp", None),
        P("section", None),
        P("section", "fsdp", None),
        P("section", "fsdp", None),
        P("section", "fsdp", None),
        P("section", None),
        P(),
    )
    out_specs = (
        P("section", "fsdp", None),
        P("section", "fsdp", None),
        P("section", "fsdp", None),
        P("section", "fsdp", None),
    )
    return jax.shard_map(shards, mesh=mesh, in_specs=in_specs, out_specs=out_specs, check_vma=False)
```
